32 devices in a mesh: blk: 8 (over z, core), rep: 4 (over y, x).
Axes of the slice: x: 2, y: 2, z: 4, core: 2. Of those that a mesh axis runs over, the one named last changes fastest.
Arguments:
- features: bfloat16 [32768, 256], P('blk'), may hold values from -6 to 6
- state: bfloat16 [32768, 256], P('blk'), may hold values from -1 to 1
- tiles: bfloat16 [8, 8, 64, 128, 128], P('blk', 'rep'), may hold values from -0.25 to 0.25
- tile_count: int32 [8, 8], P('blk', 'rep'), may hold values from 0 to 64, as said below
- tile_rows: int32 [8, 8, 64], P('blk', 'rep'), may hold values from 0 to 31, as said below
- tile_cols: int32 [8, 8, 64], P('blk', 'rep'), may hold values from 0 to 31, as said below
- w_graph: bfloat16 [256, 256], replicated, may hold values from -0.375 to 0.375
- b_graph: float32 [256], replicated, may hold values from -1 to 1
- w_input: bfloat16 [256, 768], replicated, may hold values from -0.375 to 0.375
- w_state: bfloat16 [256, 512], replicated, may hold values from -0.375 to 0.375
- w_cand: bfloat16 [256, 256], replicated, may hold values from -0.375 to 0.375
- b_gates: float32 [768], replicated, may hold values from -1 to 1
- cotangent: bfloat16 [32768, 256], P('blk'), may hold values from -6 to 6
Outputs:
- new_state: bfloat16 [32768, 256], P('blk')
- state_grad: bfloat16 [32768, 256], P('blk')
- grad_graph: float32 [256, 256], replicated
- grad_graph_bias: float32 [256], replicated
- grad_input: float32 [256, 768], replicated
- grad_state: float32 [256, 512], replicated
- grad_cand: float32 [256, 256], replicated
- grad_gates: float32 [768], replicated
The draws below stay inside these ranges and needn't reach their ends.
Inputs may be any that keep to these rules, and one draw needn't show every extreme that they name: Only the first tile_count[b, s] entries of a section list are used; some list holds exactly 64 tiles in every draw, and some lists are empty. `tile_rows`: row tile of a list entry; the (row, column) positions within one list are distinct. `tile_cols`: column tile of a list entry within its section's block of nodes.
All inputs are finite; a program needn't handle non-finite values.
Results may differ from the reference program's by a relative error of at most 0.02.
Values may be sent and summed in bfloat16 or wider, within the bound.
A program may use at most 128 MiB of HBM per device.

```python
import jax
import jax.numpy as jnp
from jax import lax

F = 256
HID = 256
TILE = 128
TR = 32
ROWS = 4096
MAXS = 64
NODES = 32768
N_BLK = 8


def tile_layout(key):
    key_level, key_count, key_blank, key_full, key_pos = jax.random.split(key, 5)
    load_level = 2 ** jax.random.randint(key_level, (N_BLK, 1), 0, 4)
    least_len = load_level * MAXS // 16
    most_len = load_level * MAXS // 8 + 1
    list_len = jax.random.randint(key_count, (N_BLK, N_BLK), least_len, most_len)
    list_len = jnp.minimum(list_len, MAXS)
    blank = (jax.random.randint(key_blank, (N_BLK, N_BLK), 0, 4) == 0).astype(jnp.int32)
    list_len = list_len * (1 - blank)
    full_at = jax.random.randint(key_full, (2,), 0, N_BLK)
    list_len = list_len.at[full_at[0], full_at[1]].set(MAXS)
    perm_keys = jax.random.split(key_pos, N_BLK * N_BLK)
    positions = jax.vmap(lambda one_key: jax.random.permutation(one_key, TR * TR))(perm_keys)
    positions = positions[:, :MAXS].reshape(N_BLK, N_BLK, MAXS).astype(jnp.int32)
    return (list_len.astype(jnp.int32), positions // TR, positions % TR)


def draw_tile_count(key, part):
    return tile_layout(key)[0]


def draw_tile_rows(key, part):
    return tile_layout(key)[1]


def draw_tile_cols(key, part):
    return tile_layout(key)[2]


def steps_of(key, dims, cuts, smallest, largest):
    gain = 1.0
    for dim, parts in cuts:
        steps = jax.random.uniform(jax.random.fold_in(jax.random.fold_in(key, 6), dim), (parts,), jnp.float32, smallest / len(cuts), largest / len(cuts))
        gain = gain * jnp.repeat(jnp.exp(steps), dims[dim] // parts).reshape((-1,) + (1,) * (len(dims) - 1 - dim))
    return gain


def noise(key, shape, deviation, bound, cuts=(), kind=jnp.bfloat16):
    level = steps_of(key, shape, cuts, -0.22, 0.18) if cuts else 1.0
    array = jax.random.normal(key, shape, jnp.float32) * deviation * level
    return jnp.minimum(jnp.maximum(array, -bound), bound).astype(kind)


def setup_inputs(seed: int = 0) -> dict:
    streams_of = jax.random.split(jax.random.key(seed), 14)
    return {
        "features": noise(streams_of[0], (NODES, F), 1.0, 6.0, ((0, 8),)),
        "state": jnp.clip(jax.random.uniform(streams_of[1], (NODES, HID), jnp.float32, -1.0, 1.0) * steps_of(streams_of[1], (NODES, HID), ((0, 8),), -0.4, 0.0), -1.0, 1.0).astype(jnp.bfloat16),
        "tiles": noise(streams_of[2], (N_BLK, N_BLK, MAXS, TILE, TILE), (TILE * N_BLK // 2) ** -0.5, 0.25, ((0, 8), (1, 4))),
        "tile_count": draw_tile_count(jax.random.fold_in(streams_of[13], 71), 0),
        "tile_rows": draw_tile_rows(jax.random.fold_in(streams_of[13], 71), 0),
        "tile_cols": draw_tile_cols(jax.random.fold_in(streams_of[13], 71), 0),
        "w_graph": noise(streams_of[6], (F, HID), F ** -0.5, 0.375),
        "b_graph": jnp.clip(jax.random.uniform(streams_of[7], (HID,), jnp.float32, -1.0, 1.0), -1.0, 1.0),
        "w_input": noise(streams_of[8], (HID, 3 * HID), HID ** -0.5, 0.375),
        "w_state": noise(streams_of[9], (HID, 2 * HID), HID ** -0.5, 0.375),
        "w_cand": noise(streams_of[10], (HID, HID), HID ** -0.5, 0.375),
        "b_gates": jnp.clip(jax.random.uniform(streams_of[11], (3 * HID,), jnp.float32, -1.0, 1.0), -1.0, 1.0),
        "cotangent": noise(streams_of[12], (NODES, HID), 1.0, 6.0, ((0, 8),)),
    }


def contract_first(left, right):
    return lax.dot_general(left, right, (((0,), (0,)), ((), ())), preferred_element_type=jnp.float32)


def contract_last(left, right):
    return lax.dot_general(left, right, (((1,), (1,)), ((), ())), preferred_element_type=jnp.float32)


def cell_step(summed, state, cotangent, w_graph, b_graph, w_input, w_state, w_cand, b_gates):
    width = w_cand.shape[0]
    summed_b = summed.astype(jnp.bfloat16)
    preact = jnp.dot(summed_b, w_graph, preferred_element_type=jnp.float32) + b_graph
    graph_out = jnp.tanh(preact)
    graph_b = graph_out.astype(jnp.bfloat16)
    from_input = jnp.dot(graph_b, w_input, preferred_element_type=jnp.float32) + b_gates
    from_state = jnp.dot(state, w_state, preferred_element_type=jnp.float32)
    reset_gate = jax.nn.sigmoid(from_input[:, :width] + from_state[:, :width])
    update_gate = jax.nn.sigmoid(from_input[:, width:2 * width] + from_state[:, width:])
    state_f = state.astype(jnp.float32)
    reset_state = (reset_gate * state_f).astype(jnp.bfloat16)
    candidate = jnp.tanh(from_input[:, 2 * width:] + jnp.dot(reset_state, w_cand, preferred_element_type=jnp.float32))
    new_state = update_gate * state_f + (1.0 - update_gate) * candidate
    upstream = cotangent.astype(jnp.float32)
    grad_update = upstream * (state_f - candidate) * update_gate * (1.0 - update_gate)
    grad_cand_f = upstream * (1.0 - update_gate) * (1.0 - candidate * candidate)
    grad_cand_b = grad_cand_f.astype(jnp.bfloat16)
    grad_reset_state = contract_last(grad_cand_b, w_cand)
    grad_reset = grad_reset_state * state_f * reset_gate * (1.0 - reset_gate)
    gate_grads = jnp.concatenate([grad_reset.astype(jnp.bfloat16), grad_update.astype(jnp.bfloat16), grad_cand_b], axis=1)
    gate_sums = jnp.concatenate([jnp.sum(grad_reset, axis=0), jnp.sum(grad_update, axis=0), jnp.sum(grad_cand_f, axis=0)])
    grad_input = contract_first(graph_b, gate_grads)
    grad_state = contract_first(state, gate_grads[:, :2 * width])
    grad_cand = contract_first(reset_state, grad_cand_b)
    grad_graph_out = contract_last(gate_grads, w_input)
    grad_preact = grad_graph_out * (1.0 - graph_out * graph_out)
    grad_graph = contract_first(summed_b, grad_preact.astype(jnp.bfloat16))
    graph_bias_sum = jnp.sum(grad_preact, axis=0)
    state_grad = upstream * update_gate + grad_reset_state * reset_gate + contract_last(gate_grads[:, :2 * width], w_state)
    return new_state.astype(jnp.bfloat16), state_grad.astype(jnp.bfloat16), (grad_graph, graph_bias_sum, grad_input, grad_state, grad_cand, gate_sums)


def reference(features, state, tiles, tile_count, tile_rows, tile_cols, w_graph, b_graph, w_input, w_state, w_cand, b_gates, cotangent):
    feat_tiles = features.reshape(N_BLK, TR, TILE, F).astype(jnp.float32)
    section_ids = jnp.arange(N_BLK, dtype=jnp.int32)
    entry_ids = jnp.arange(MAXS, dtype=jnp.int32)
    row_ids = jnp.arange(TR, dtype=jnp.int32)

    def block_sum(inputs):
        block_tiles, block_count, block_rows, block_cols = inputs
        picked = feat_tiles[section_ids[:, None], block_cols]
        products = jnp.einsum("smab,smbf->smaf", block_tiles.astype(jnp.float32), picked)
        in_list = entry_ids[None, :] < block_count[:, None]
        placing = ((block_rows[:, :, None] == row_ids[None, None, :]) & in_list[:, :, None]).astype(jnp.float32)
        return jnp.einsum("smr,smaf->raf", placing, products).reshape(ROWS, F)

    summed = lax.map(block_sum, (tiles, tile_count, tile_rows, tile_cols)).reshape(NODES, F)
    new_state, state_grad, grads = cell_step(summed, state, cotangent, w_graph, b_graph, w_input, w_state, w_cand, b_gates)
    scale = NODES ** -0.5
    grad_graph, graph_bias_sum, grad_input, grad_state, grad_cand, gate_sums = grads
    return (new_state, state_grad, grad_graph * scale, graph_bias_sum * scale, grad_input * scale,
            grad_state * scale, grad_cand * scale, gate_sums * scale)
```

```python
import functools

import jax
import jax.numpy as jnp
from jax import lax
from jax.experimental import pallas as pl
from jax.experimental.pallas import tpu as pltpu
from jax.sharding import PartitionSpec as P

MESH = pl.DeviceIdType.MESH
CHUNKS = 32
WINDOW = 4
GROUP = 8
ROW_BLOCK = 256
VMEM_LIMIT = 56 * 1024 * 1024


def contract_first(left, right):
    return lax.dot_general(
        left, right, (((0,), (0,)), ((), ())), preferred_element_type=jnp.float32
    )


def contract_last(left, right):
    return lax.dot_general(
        left, right, (((1,), (1,)), ((), ())), preferred_element_type=jnp.float32
    )


def product(left, right):
    return jnp.dot(left, right, preferred_element_type=jnp.float32)


def spread_kernel(chips, feat, out, up_sem, down_sem, recv_sem, pair_sem, pair_recv, own_sem):
    blk = lax.axis_index("blk")
    rep = lax.axis_index("rep")
    core = blk % 2
    chip = blk // 2
    above = (chip + 1) % chips
    below = (chip + chips - 1) % chips
    chunk = feat.shape[0] // CHUNKS

    barrier = pltpu.get_barrier_semaphore()
    for other in (above * 2 + core, below * 2 + core, chip * 2 + 1 - core):
        pl.semaphore_signal(
            barrier, inc=1, device_id={"blk": other, "rep": rep}, device_id_type=MESH
        )
    pl.semaphore_wait(barrier, 3)

    def rows_of(j):
        return pl.ds(pl.multiple_of(j * chunk, chunk), chunk)

    def send(src, j, target, send_sem, recv):
        return pltpu.make_async_remote_copy(
            src_ref=src,
            dst_ref=out.at[core, rows_of(j)],
            send_sem=send_sem.at[j],
            recv_sem=recv.at[j],
            device_id={"blk": target, "rep": rep},
            device_id_type=MESH,
        )

    def up(src, j):
        return send(src, j, above * 2 + core, up_sem, recv_sem)

    def down(src, j):
        return send(src, j, below * 2 + core, down_sem, recv_sem)

    def pair(src, j):
        return send(src, j, chip * 2 + 1 - core, pair_sem, pair_recv)

    has_up = jnp.logical_and(chip >= rep, chip < chips - 1)
    has_down = jnp.logical_and(chip <= rep, chip > 0)
    is_owner = chip == rep

    @pl.when(is_owner)
    def _():
        own = pltpu.make_async_copy(feat, out.at[core], own_sem)
        own.start()

        def step(j, carry):
            src = feat.at[rows_of(j)]

            @pl.when(has_up)
            def _():
                @pl.when(j >= WINDOW)
                def _():
                    up(feat.at[rows_of(j - WINDOW)], j - WINDOW).wait_send()

                up(src, j).start()

            @pl.when(has_down)
            def _():
                @pl.when(j >= WINDOW)
                def _():
                    down(feat.at[rows_of(j - WINDOW)], j - WINDOW).wait_send()

                down(src, j).start()

            pair(src, j).start()
            return carry

        lax.fori_loop(0, CHUNKS, step, 0)

        def finish(j, carry):
            src = feat.at[rows_of(j)]

            @pl.when(jnp.logical_and(has_up, j >= CHUNKS - WINDOW))
            def _():
                up(src, j).wait_send()

            @pl.when(jnp.logical_and(has_down, j >= CHUNKS - WINDOW))
            def _():
                down(src, j).wait_send()

            pair(src, j).wait()
            return carry

        lax.fori_loop(0, CHUNKS, finish, 0)
        own.wait()

    @pl.when(jnp.logical_not(is_owner))
    def _():
        def step(j, carry):
            src = out.at[core, rows_of(j)]
            up(src, j).wait_recv()

            @pl.when(has_up)
            def _():
                up(src, j).start()

            @pl.when(has_down)
            def _():
                down(src, j).start()

            pair(src, j).start()
            return carry

        lax.fori_loop(0, CHUNKS, step, 0)

        def finish(j, carry):
            src = out.at[core, rows_of(j)]

            @pl.when(has_up)
            def _():
                up(src, j).wait_send()

            @pl.when(has_down)
            def _():
                down(src, j).wait_send()

            pair(src, j).wait()
            return carry

        lax.fori_loop(0, CHUNKS, finish, 0)


def spread(features, chips, per_rep):
    dma = pltpu.SemaphoreType.DMA((CHUNKS,))
    return pl.pallas_call(
        functools.partial(spread_kernel, chips),
        out_shape=jax.ShapeDtypeStruct((per_rep,) + features.shape, features.dtype),
        in_specs=[pl.BlockSpec(memory_space=pl.ANY)],
        out_specs=pl.BlockSpec(memory_space=pl.ANY),
        scratch_shapes=[dma, dma, dma, dma, dma, pltpu.SemaphoreType.DMA(())],
        compiler_params=pltpu.CompilerParams(
            collective_id=0, has_side_effects=True, vmem_limit_bytes=VMEM_LIMIT
        ),
    )(features)


def tiles_kernel(count, rows, cols, tiles, sections, out, acc):
    slot = pl.program_id(0)
    side = tiles.shape[2]

    @pl.when(slot == 0)
    def _():
        acc[...] = jnp.zeros_like(acc)

    used = count[0, slot]

    def step(g, carry):
        terms = []
        for i in range(GROUP):
            m = g * GROUP + i
            col = pl.multiple_of(cols[0, slot, m] * side, side)
            term = product(tiles[0, m], sections[0, pl.ds(col, side), :])
            terms.append(jnp.where(m < used, term, 0.0))
        for i in range(GROUP):
            row = pl.multiple_of(rows[0, slot, g * GROUP + i] * side, side)
            acc[pl.ds(row, side), :] += terms[i]
        return carry

    lax.fori_loop(0, (used + GROUP - 1) // GROUP, step, 0)

    @pl.when(slot == pl.num_programs(0) - 1)
    def _():
        out[...] = acc[...].astype(out.dtype)


def tile_products(count, rows, cols, tiles, sections):
    per_rep, cap, side = tiles.shape[:3]
    node_rows, width = sections.shape[1:]
    return pl.pallas_call(
        tiles_kernel,
        out_shape=jax.ShapeDtypeStruct((node_rows, width), jnp.bfloat16),
        grid_spec=pltpu.PrefetchScalarGridSpec(
            num_scalar_prefetch=3,
            grid=(per_rep,),
            in_specs=[
                pl.BlockSpec((1, cap, side, side), lambda s, *_: (s, 0, 0, 0)),
                pl.BlockSpec((1, node_rows, width), lambda s, *_: (s, 0, 0)),
            ],
            out_specs=pl.BlockSpec((node_rows, width), lambda s, *_: (0, 0)),
            scratch_shapes=[pltpu.VMEM((node_rows, width), jnp.float32)],
        ),
        compiler_params=pltpu.CompilerParams(vmem_limit_bytes=VMEM_LIMIT),
    )(count, rows, cols, tiles, sections)


def cell_kernel(
    chips,
    reps,
    scale,
    partial,
    state_hbm,
    cot_hbm,
    w_graph,
    b_graph,
    w_input,
    w_state,
    w_cand,
    b_gates,
    new_state,
    state_grad,
    grad_graph,
    graph_bias,
    grad_input,
    grad_state,
    grad_cand,
    gate_sums,
    state_v,
    cot_v,
    s_all,
    part_own,
    part_recv,
    grads,
    grads_b,
    half_recv,
    half_b,
    chip_recv,
    rep_recv,
    final,
    local_sem,
    rs_send,
    rs_recv,
    ag_send,
    ag_recv,
    pair_send,
    pair_recv,
    chip_send,
    chip_got,
    rep_send,
    rep_got,
    chip_send2,
    chip_got2,
):
    blk = lax.axis_index("blk")
    rep = lax.axis_index("rep")
    core = blk % 2
    chip = blk // 2
    width = w_cand.shape[0]
    part_rows = partial.shape[0] // reps
    half_rows = half_b.shape[0]
    piece_rows = rep_recv.shape[1]
    weight_rows = 7 * width

    def rep_at(k):
        return ((rep // 2 + k // 2) % (reps // 2)) * 2 + (rep % 2 + k % 2) % 2

    def rep_from(k):
        return ((rep // 2 + reps // 2 - k // 2) % (reps // 2)) * 2 + (rep % 2 + k % 2) % 2

    def on_rep(k):
        return {"blk": blk, "rep": rep_at(k)}

    def chip_at(k):
        return (chip + k) % chips

    def on_chip(k):
        return {"blk": chip_at(k) * 2 + core, "rep": rep}

    mate = {"blk": chip * 2 + 1 - core, "rep": rep}

    def part(index):
        return pl.ds(pl.multiple_of(index * part_rows, part_rows), part_rows)

    def piece(index):
        return pl.ds(pl.multiple_of(index * piece_rows, piece_rows), piece_rows)

    def half(index):
        return pl.ds(pl.multiple_of(index * half_rows, half_rows), half_rows)

    def remote(src, dst, send_sem, recv_sem, target):
        return pltpu.make_async_remote_copy(
            src_ref=src,
            dst_ref=dst,
            send_sem=send_sem,
            recv_sem=recv_sem,
            device_id=target,
            device_id_type=MESH,
        )

    loads = [
        pltpu.make_async_copy(partial.at[part(rep)], part_own, local_sem.at[0]),
        pltpu.make_async_copy(state_hbm, state_v, local_sem.at[1]),
        pltpu.make_async_copy(cot_hbm, cot_v, local_sem.at[2]),
    ]
    for load in loads:
        load.start()

    barrier = pltpu.get_barrier_semaphore()
    targets = [on_rep(k) for k in range(1, reps)] + [on_chip(k) for k in range(1, chips)] + [mate]
    for target in targets:
        pl.semaphore_signal(barrier, inc=1, device_id=target, device_id_type=MESH)
    pl.semaphore_wait(barrier, len(targets))

    scatter = [
        remote(
            partial.at[part(rep_at(k))],
            part_recv.at[k - 1],
            rs_send.at[k - 1],
            rs_recv.at[k - 1],
            on_rep(k),
        )
        for k in range(1, reps)
    ]
    for copy in reversed(scatter):
        copy.start()
    grads[...] = jnp.zeros_like(grads)
    for load in loads:
        load.wait()
    for copy in scatter:
        copy.wait()

    own_base = rep * part_rows

    def add_up(i, carry):
        here = pl.ds(pl.multiple_of(i * ROW_BLOCK, ROW_BLOCK), ROW_BLOCK)
        total = part_own[here, :].astype(jnp.float32)
        for k in range(reps - 1):
            total = total + part_recv[k, here, :].astype(jnp.float32)
        there = pl.ds(pl.multiple_of(own_base + i * ROW_BLOCK, ROW_BLOCK), ROW_BLOCK)
        s_all[there, :] = total.astype(jnp.bfloat16)
        return carry

    lax.fori_loop(0, part_rows // ROW_BLOCK, add_up, 0)

    gather = [
        remote(
            s_all.at[part(rep)],
            s_all.at[part(rep)],
            ag_send.at[k - 1],
            ag_recv.at[k - 1],
            on_rep(k),
        )
        for k in range(1, reps)
    ]
    for copy in gather:
        copy.start()

    def cell(base, with_grads):
        def step(i, carry):
            here = pl.ds(pl.multiple_of(base + i * ROW_BLOCK, ROW_BLOCK), ROW_BLOCK)
            summed_b = s_all[here, :]
            state = state_v[here, :]
            graph_out = jnp.tanh(product(summed_b, w_graph[...]) + b_graph[...])
            graph_b = graph_out.astype(jnp.bfloat16)
            from_input = product(graph_b, w_input[...]) + b_gates[...]
            from_state = product(state, w_state[...])
            reset_gate = jax.nn.sigmoid(from_input[:, :width] + from_state[:, :width])
            update_gate = jax.nn.sigmoid(from_input[:, width : 2 * width] + from_state[:, width:])
            state_f = state.astype(jnp.float32)
            reset_state = (reset_gate * state_f).astype(jnp.bfloat16)
            candidate = jnp.tanh(from_input[:, 2 * width :] + product(reset_state, w_cand[...]))
            keep = 1.0 - update_gate
            new_state[here, :] = (update_gate * state_f + keep * candidate).astype(jnp.bfloat16)
            upstream = cot_v[here, :].astype(jnp.float32)
            grad_update = upstream * (state_f - candidate) * update_gate * keep
            grad_cand_f = upstream * keep * (1.0 - candidate * candidate)
            grad_cand_b = grad_cand_f.astype(jnp.bfloat16)
            grad_reset_state = contract_last(grad_cand_b, w_cand[...])
            grad_reset = grad_reset_state * state_f * reset_gate * (1.0 - reset_gate)
            gates_b = jnp.concatenate(
                [grad_reset.astype(jnp.bfloat16), grad_update.astype(jnp.bfloat16)], axis=1
            )
            state_grad[here, :] = (
                upstream * update_gate
                + grad_reset_state * reset_gate
                + contract_last(gates_b, w_state[...])
            ).astype(jnp.bfloat16)
            if with_grads:
                all_b = jnp.concatenate([gates_b, grad_cand_b], axis=1)
                grad_preact = contract_last(all_b, w_input[...]) * (1.0 - graph_out * graph_out)

                def add(at, value):
                    rows = pl.ds(at, value.shape[0])
                    grads[rows, :] += value

                add(0, contract_first(summed_b, grad_preact.astype(jnp.bfloat16)))
                to_input = contract_first(graph_b, all_b)
                for n in range(3):
                    add((1 + n) * width, to_input[:, n * width : (n + 1) * width])
                to_state = contract_first(state, gates_b)
                for n in range(2):
                    add((4 + n) * width, to_state[:, n * width : (n + 1) * width])
                add(6 * width, contract_first(reset_state, grad_cand_b))
                sums = [
                    jnp.sum(term, axis=0, keepdims=True)
                    for term in (grad_preact, grad_reset, grad_update, grad_cand_f)
                ]
                add(weight_rows, jnp.concatenate(sums + [jnp.zeros((4, width), jnp.float32)]))
            return carry

        lax.fori_loop(0, part_rows // ROW_BLOCK, step, 0)

    cell(own_base, True)

    to_mate = remote(
        grads_b.at[half(1 - core)], half_recv, pair_send.at[0], pair_recv.at[0], mate
    )
    between = [
        remote(
            half_b.at[piece(chip_at(k))],
            chip_recv.at[k - 1],
            chip_send.at[k - 1],
            chip_got.at[k - 1],
            on_chip(k),
        )
        for k in range(1, chips)
    ]
    across = [
        remote(
            rep_recv.at[rep], rep_recv.at[rep], rep_send.at[k - 1], rep_got.at[k - 1], on_rep(k)
        )
        for k in range(1, reps)
    ]
    mine = piece(core * chips + chip)
    back = [
        remote(
            final.at[mine], final.at[mine], chip_send2.at[k - 1], chip_got2.at[k - 1], on_chip(k)
        )
        for k in range(1, chips)
    ]
    back_mate = remote(
        final.at[half(core)], final.at[half(core)], pair_send.at[1], pair_recv.at[1], mate
    )

    def stage_pair():
        to_mate.wait()
        half_b[...] = (grads[half(core), :] + half_recv[...].astype(jnp.float32)).astype(
            jnp.bfloat16
        )
        for copy in between:
            copy.start()

    def stage_chip():
        for copy in between:
            copy.wait()
        total = half_b[piece(chip), :].astype(jnp.float32)
        for k in range(chips - 1):
            total = total + chip_recv[k].astype(jnp.float32)
        rep_recv[rep] = total.astype(jnp.bfloat16)
        for copy in across:
            copy.start()

    def stage_rep():
        for copy in across:
            copy.wait()
        total = rep_recv[0].astype(jnp.float32)
        for k in range(1, reps):
            total = total + rep_recv[k].astype(jnp.float32)
        final[mine, :] = (total * scale).astype(jnp.bfloat16)
        for copy in back:
            copy.start()

    def stage_back():
        for copy in back:
            copy.wait()
        back_mate.start()

    grads_b[...] = grads[...].astype(jnp.bfloat16)
    to_mate.start()
    stages = [stage_pair, stage_chip, stage_rep, stage_back]
    for k in range(1, reps):
        gather[k - 1].wait()
        cell(rep_from(k) * part_rows, False)
        if stages:
            stages.pop(0)()
    for stage in stages:
        stage()
    back_mate.wait()

    def take(at, count):
        return final[pl.ds(at, count), :].astype(jnp.float32)

    grad_graph[...] = take(0, width)
    for n in range(3):
        grad_input[:, n * width : (n + 1) * width] = take((1 + n) * width, width)
    for n in range(2):
        grad_state[:, n * width : (n + 1) * width] = take((4 + n) * width, width)
    grad_cand[...] = take(6 * width, width)
    bias = take(weight_rows, 16)
    graph_bias[...] = bias[0:1]
    for n in range(3):
        gate_sums[:, n * width : (n + 1) * width] = bias[1 + n : 2 + n]


def cell_step(partial, state, cotangent, weights, chips, reps):
    node_rows, width = partial.shape
    blks = chips * 2
    unit = 16 * blks
    grad_rows = (7 * width + 16 + unit - 1) // unit * unit
    half_rows = grad_rows // 2
    piece_rows = grad_rows // blks
    part_rows = node_rows // reps
    scale = float(node_rows * blks) ** (-0.5)
    f32, b16 = jnp.float32, jnp.bfloat16
    shape = jax.ShapeDtypeStruct
    whole = pl.BlockSpec(memory_space=pltpu.VMEM)
    anywhere = pl.BlockSpec(memory_space=pl.ANY)
    dma = pltpu.SemaphoreType.DMA
    return pl.pallas_call(
        functools.partial(cell_kernel, chips, reps, scale),
        out_shape=[
            shape((node_rows, width), b16),
            shape((node_rows, width), b16),
            shape((width, width), f32),
            shape((1, width), f32),
            shape((width, 3 * width), f32),
            shape((width, 2 * width), f32),
            shape((width, width), f32),
            shape((1, 3 * width), f32),
        ],
        in_specs=[anywhere] * 3 + [whole] * 6,
        out_specs=[whole] * 8,
        scratch_shapes=[
            pltpu.VMEM((node_rows, width), b16),
            pltpu.VMEM((node_rows, width), b16),
            pltpu.VMEM((node_rows, width), b16),
            pltpu.VMEM((part_rows, width), b16),
            pltpu.VMEM((reps - 1, part_rows, width), b16),
            pltpu.VMEM((grad_rows, width), f32),
            pltpu.VMEM((grad_rows, width), b16),
            pltpu.VMEM((half_rows, width), b16),
            pltpu.VMEM((half_rows, width), b16),
            pltpu.VMEM((chips - 1, piece_rows, width), b16),
            pltpu.VMEM((reps, piece_rows, width), b16),
            pltpu.VMEM((grad_rows, width), b16),
            dma((3,)),
            dma((reps - 1,)),
            dma((reps - 1,)),
            dma((reps - 1,)),
            dma((reps - 1,)),
            dma((2,)),
            dma((2,)),
            dma((chips - 1,)),
            dma((chips - 1,)),
            dma((reps - 1,)),
            dma((reps - 1,)),
            dma((chips - 1,)),
            dma((chips - 1,)),
        ],
        compiler_params=pltpu.CompilerParams(
            collective_id=1, has_side_effects=True, vmem_limit_bytes=VMEM_LIMIT
        ),
    )(partial, state, cotangent, *weights)


def solution(mesh):
    chips = mesh.shape["blk"] // 2
    reps = mesh.shape["rep"]

    def local(
        features,
        state,
        tiles,
        tile_count,
        tile_rows,
        tile_cols,
        w_graph,
        b_graph,
        w_input,
        w_state,
        w_cand,
        b_gates,
        cotangent,
    ):
        sections = spread(features, chips, tiles.shape[1])
        partial = tile_products(tile_count, tile_rows, tile_cols, tiles[0], sections)
        weights = (
            w_graph,
            b_graph.reshape(1, -1),
            w_input,
            w_state,
            w_cand,
            b_gates.reshape(1, -1),
        )
        outs = cell_step(partial, state, cotangent, weights, chips, reps)
        return (
            outs[0],
            outs[1],
            outs[2],
            outs[3].reshape(-1),
            outs[4],
            outs[5],
            outs[6],
            outs[7].reshape(-1),
        )

    in_specs = (
        P("blk", None),
        P("blk", None),
        P("blk", "rep", None, None, None),
        P("blk", "rep"),
        P("blk", "rep", None),
        P("blk", "rep", None),
        P(),
        P(),
        P(),
        P(),
        P(),
        P(),
        P("blk", None),
    )
    out_specs = (P("blk", None), P("blk", None), P(), P(), P(), P(), P(), P())
    return jax.shard_map(local, mesh=mesh, in_specs=in_specs, out_specs=out_specs, check_vma=False)
```

```python
import functools

import jax
import jax.numpy as jnp
from jax import lax
from jax.experimental import pallas as pl
from jax.experimental.pallas import tpu as pltpu
from jax.sharding import PartitionSpec as P

MESH = pl.DeviceIdType.MESH
CHUNKS = 16
GROUP = 8
ROW_BLOCK = 256
VMEM_LIMIT = 56 * 1024 * 1024


def contract_first(left, right):
    return lax.dot_general(
        left, right, (((0,), (0,)), ((), ())), preferred_element_type=jnp.float32
    )


def contract_last(left, right):
    return lax.dot_general(
        left, right, (((1,), (1,)), ((), ())), preferred_element_type=jnp.float32
    )


def product(left, right):
    return jnp.dot(left, right, preferred_element_type=jnp.float32)


def rep_shift(rep, reps, k):
    return ((rep // 2 + k // 2) % (reps // 2)) * 2 + (rep % 2 + k % 2) % 2


def rep_origin(rep, reps, k):
    return ((rep // 2 + reps // 2 - k // 2) % (reps // 2)) * 2 + (rep % 2 + k % 2) % 2


def spread_kernel(chips, reps, lane, reduces, *refs):
    if reduces:
        feat, partial, out, s_all = refs[:4]
        sems = refs[4:]
        part_own, part_recv, part_sem, rs_send, rs_recv, ag_send, ag_recv = sems[6:]
    else:
        feat, out = refs[:2]
        sems = refs[2:]
    up_sem, down_sem, recv_sem, pair_sem, pair_recv, own_sem = sems[:6]
    blk = lax.axis_index("blk")
    rep = lax.axis_index("rep")
    core = blk % 2
    chip = blk // 2
    above = (chip + 1) % chips
    below = (chip + chips - 1) % chips
    chunk = feat.shape[0] // CHUNKS
    lanes = out.shape[2]
    is_owner = chip == rep
    not_owner = chip != rep
    has_up = jnp.logical_and(chip >= rep, chip < chips - 1)
    has_down = jnp.logical_and(chip <= rep, chip > 0)

    def rows_of(j):
        return pl.ds(pl.multiple_of(j * chunk, chunk), chunk)

    def own(j):
        return pltpu.make_async_copy(
            feat.at[rows_of(j), pl.ds(lane, lanes)], out.at[core, rows_of(j)], own_sem.at[j]
        )

    def load(j, carry):
        own(j).start()
        return carry

    @pl.when(is_owner)
    def _():
        lax.fori_loop(0, CHUNKS, load, 0)

    def remote(src, dst, send_sem, recv_sem, target):
        return pltpu.make_async_remote_copy(
            src_ref=src,
            dst_ref=dst,
            send_sem=send_sem,
            recv_sem=recv_sem,
            device_id=target,
            device_id_type=MESH,
        )

    def send(j, target, send_sem, got):
        here = out.at[core, rows_of(j)]
        return remote(here, here, send_sem.at[j], got.at[j], {"blk": target, "rep": rep})

    def up(j):
        return send(j, above * 2 + core, up_sem, recv_sem)

    def down(j):
        return send(j, below * 2 + core, down_sem, recv_sem)

    def pair(j):
        return send(j, chip * 2 + 1 - core, pair_sem, pair_recv)

    others = range(1, reps)
    targets = [
        {"blk": other, "rep": rep}
        for other in (above * 2 + core, below * 2 + core, chip * 2 + 1 - core)
    ]
    if reduces:
        targets += [{"blk": blk, "rep": rep_shift(rep, reps, k)} for k in others]
    barrier = pltpu.get_barrier_semaphore()
    for target in targets:
        pl.semaphore_signal(barrier, inc=1, device_id=target, device_id_type=MESH)
    pl.semaphore_wait(barrier, len(targets))

    if reduces:
        part_rows = partial.shape[0] // reps

        def part(index):
            return pl.ds(pl.multiple_of(index * part_rows, part_rows), part_rows)

        load_own = pltpu.make_async_copy(partial.at[part(rep)], part_own, part_sem)
        load_own.start()
        scatter = [
            remote(
                partial.at[part(rep_shift(rep, reps, k))],
                part_recv.at[k - 1],
                rs_send.at[k - 1],
                rs_recv.at[k - 1],
                {"blk": blk, "rep": rep_shift(rep, reps, k)},
            )
            for k in others
        ]
        gather = [
            remote(
                s_all.at[part(rep)],
                s_all.at[part(rep)],
                ag_send.at[k - 1],
                ag_recv.at[k - 1],
                {"blk": blk, "rep": rep_shift(rep, reps, k)},
            )
            for k in others
        ]
        for copy in reversed(scatter):
            copy.start()

    def step(j, carry):
        @pl.when(is_owner)
        def _():
            own(j).wait()

        @pl.when(not_owner)
        def _():
            up(j).wait_recv()

        @pl.when(has_up)
        def _():
            up(j).start()

        @pl.when(has_down)
        def _():
            down(j).start()

        pair(j).start()
        return carry

    middle = CHUNKS * 5 // 8 if reduces else CHUNKS
    lax.fori_loop(0, middle, step, 0)
    if reduces:
        load_own.wait()
        for copy in scatter:
            copy.wait()
        add_parts(part_own, part_recv, s_all, rep * part_rows)
        for copy in gather:
            copy.start()
        lax.fori_loop(middle, CHUNKS, step, 0)

    def finish(j, carry):
        @pl.when(has_up)
        def _():
            up(j).wait_send()

        @pl.when(has_down)
        def _():
            down(j).wait_send()

        pair(j).wait()
        return carry

    lax.fori_loop(0, CHUNKS, finish, 0)
    if reduces:
        for copy in gather:
            copy.wait()


def add_parts(part_own, part_recv, s_all, base):
    others, rows = part_recv.shape[:2]

    def step(i, carry):
        here = pl.ds(pl.multiple_of(i * ROW_BLOCK, ROW_BLOCK), ROW_BLOCK)
        total = part_own[here, :].astype(jnp.float32)
        for k in range(others):
            total = total + part_recv[k, here, :].astype(jnp.float32)
        there = pl.ds(pl.multiple_of(base + i * ROW_BLOCK, ROW_BLOCK), ROW_BLOCK)
        s_all[there, :] = total.astype(jnp.bfloat16)
        return carry

    lax.fori_loop(0, rows // ROW_BLOCK, step, 0)


def spread(features, partial, lane, chips, reps, per_rep):
    reduces = partial is not None
    node_rows, width = features.shape
    lanes = width // 2
    part_rows = node_rows // reps
    chunk_sem = pltpu.SemaphoreType.DMA((CHUNKS,))
    rep_sem = pltpu.SemaphoreType.DMA((reps - 1,))
    shape = jax.ShapeDtypeStruct
    anywhere = pl.BlockSpec(memory_space=pl.ANY)
    vmem = pl.BlockSpec(memory_space=pltpu.VMEM)
    args = [features]
    out_shape = [shape((per_rep, node_rows, lanes), features.dtype)]
    scratch = [chunk_sem] * 6
    if reduces:
        args.append(partial)
        out_shape.append(shape((node_rows, lanes), features.dtype))
        scratch += [
            pltpu.VMEM((part_rows, lanes), jnp.bfloat16),
            pltpu.VMEM((reps - 1, part_rows, lanes), jnp.bfloat16),
            pltpu.SemaphoreType.DMA(()),
            rep_sem,
            rep_sem,
            rep_sem,
            rep_sem,
        ]
    return pl.pallas_call(
        functools.partial(spread_kernel, chips, reps, lane, reduces),
        out_shape=out_shape,
        in_specs=[anywhere] * len(args),
        out_specs=[vmem] * len(out_shape),
        scratch_shapes=scratch,
        compiler_params=pltpu.CompilerParams(
            collective_id=2 if reduces else 0, has_side_effects=True, vmem_limit_bytes=VMEM_LIMIT
        ),
    )(*args)


def tiles_kernel(count, rows, cols, tiles, sections, out, acc):
    slot = pl.program_id(0)
    side = tiles.shape[2]

    @pl.when(slot == 0)
    def _():
        acc[...] = jnp.zeros_like(acc)

    used = count[0, slot]

    def step(g, carry):
        terms = []
        for i in range(GROUP):
            m = g * GROUP + i
            col = pl.multiple_of(cols[0, slot, m] * side, side)
            term = product(tiles[0, m], sections[0, pl.ds(col, side), :])
            terms.append(jnp.where(m < used, term, 0.0))
        for i in range(GROUP):
            row = pl.multiple_of(rows[0, slot, g * GROUP + i] * side, side)
            acc[pl.ds(row, side), :] += terms[i]
        return carry

    lax.fori_loop(0, (used + GROUP - 1) // GROUP, step, 0)

    @pl.when(slot == pl.num_programs(0) - 1)
    def _():
        out[...] = acc[...].astype(out.dtype)


def tile_products(count, rows, cols, tiles, sections):
    per_rep, cap, side = tiles.shape[:3]
    node_rows, width = sections.shape[1:]
    return pl.pallas_call(
        tiles_kernel,
        out_shape=jax.ShapeDtypeStruct((node_rows, width), jnp.bfloat16),
        grid_spec=pltpu.PrefetchScalarGridSpec(
            num_scalar_prefetch=3,
            grid=(per_rep,),
            in_specs=[
                pl.BlockSpec((1, cap, side, side), lambda s, *_: (s, 0, 0, 0)),
                pl.BlockSpec((1, node_rows, width), lambda s, *_: (s, 0, 0)),
            ],
            out_specs=pl.BlockSpec((node_rows, width), lambda s, *_: (0, 0)),
            scratch_shapes=[pltpu.VMEM((node_rows, width), jnp.float32)],
        ),
        compiler_params=pltpu.CompilerParams(vmem_limit_bytes=VMEM_LIMIT),
    )(count, rows, cols, tiles, sections)


def cell_kernel(
    chips,
    reps,
    scale,
    partial,
    first_half,
    state_hbm,
    cot_hbm,
    w_graph,
    b_graph,
    w_input,
    w_state,
    w_cand,
    b_gates,
    new_state,
    state_grad,
    grads_out,
    state_v,
    cot_v,
    s_all,
    part_own,
    part_recv,
    grads,
    grads_b,
    half_recv,
    half_b,
    rep_recv,
    quarter_b,
    chip_recv,
    final,
    local_sem,
    rs_send,
    rs_recv,
    ag_send,
    ag_recv,
    pair_send,
    pair_recv,
    chip_send,
    chip_got,
    rep_send,
    rep_got,
    chip_send2,
    chip_got2,
    rep_send2,
    rep_got2,
):
    blk = lax.axis_index("blk")
    rep = lax.axis_index("rep")
    core = blk % 2
    chip = blk // 2
    width = w_cand.shape[0]
    part_rows = partial.shape[0] // reps
    half_rows = half_b.shape[0]
    quarter_rows = quarter_b.shape[0]
    piece_rows = chip_recv.shape[1]
    weight_rows = 7 * width

    def rep_at(k):
        return rep_shift(rep, reps, k)

    def on_rep(k):
        return {"blk": blk, "rep": rep_at(k)}

    def chip_at(k):
        return (chip + k) % chips

    def on_chip(k):
        return {"blk": chip_at(k) * 2 + core, "rep": rep}

    mate = {"blk": chip * 2 + 1 - core, "rep": rep}

    def part(index):
        return pl.ds(pl.multiple_of(index * part_rows, part_rows), part_rows)

    def piece(index):
        return pl.ds(pl.multiple_of(index * piece_rows, piece_rows), piece_rows)

    def quarter(index):
        return pl.ds(pl.multiple_of(index * quarter_rows, quarter_rows), quarter_rows)

    def half(index):
        return pl.ds(pl.multiple_of(index * half_rows, half_rows), half_rows)

    def remote(src, dst, send_sem, recv_sem, target):
        return pltpu.make_async_remote_copy(
            src_ref=src,
            dst_ref=dst,
            send_sem=send_sem,
            recv_sem=recv_sem,
            device_id=target,
            device_id_type=MESH,
        )

    loads = [
        pltpu.make_async_copy(partial.at[part(rep)], part_own, local_sem.at[0]),
        pltpu.make_async_copy(state_hbm, state_v, local_sem.at[1]),
        pltpu.make_async_copy(cot_hbm, cot_v, local_sem.at[2]),
    ]
    for load in loads:
        load.start()

    barrier = pltpu.get_barrier_semaphore()
    targets = [on_rep(k) for k in range(1, reps)] + [on_chip(k) for k in range(1, chips)] + [mate]
    for target in targets:
        pl.semaphore_signal(barrier, inc=1, device_id=target, device_id_type=MESH)
    pl.semaphore_wait(barrier, len(targets))

    scatter = [
        remote(
            partial.at[part(rep_at(k))],
            part_recv.at[k - 1],
            rs_send.at[k - 1],
            rs_recv.at[k - 1],
            on_rep(k),
        )
        for k in range(1, reps)
    ]
    for copy in reversed(scatter):
        copy.start()
    grads[...] = jnp.zeros_like(grads)
    for load in loads:
        load.wait()
    for copy in scatter:
        copy.wait()

    own_base = rep * part_rows
    add_parts(part_own, part_recv, s_all, own_base)

    gather = [
        remote(
            s_all.at[part(rep)],
            s_all.at[part(rep)],
            ag_send.at[k - 1],
            ag_recv.at[k - 1],
            on_rep(k),
        )
        for k in range(1, reps)
    ]
    for copy in gather:
        copy.start()

    def cell(base, with_grads):
        def step(i, carry):
            here = pl.ds(pl.multiple_of(base + i * ROW_BLOCK, ROW_BLOCK), ROW_BLOCK)
            summed_b = jnp.concatenate([first_half[here, :], s_all[here, :]], axis=1)
            state = state_v[here, :]
            graph_out = jnp.tanh(product(summed_b, w_graph[...]) + b_graph[...].reshape(1, -1))
            graph_b = graph_out.astype(jnp.bfloat16)
            from_input = product(graph_b, w_input[...]) + b_gates[...].reshape(1, -1)
            from_state = product(state, w_state[...])
            reset_gate = jax.nn.sigmoid(from_input[:, :width] + from_state[:, :width])
            update_gate = jax.nn.sigmoid(from_input[:, width : 2 * width] + from_state[:, width:])
            state_f = state.astype(jnp.float32)
            reset_state = (reset_gate * state_f).astype(jnp.bfloat16)
            candidate = jnp.tanh(from_input[:, 2 * width :] + product(reset_state, w_cand[...]))
            keep = 1.0 - update_gate
            new_state[here, :] = (update_gate * state_f + keep * candidate).astype(jnp.bfloat16)
            upstream = cot_v[here, :].astype(jnp.float32)
            grad_update = upstream * (state_f - candidate) * update_gate * keep
            grad_cand_f = upstream * keep * (1.0 - candidate * candidate)
            grad_cand_b = grad_cand_f.astype(jnp.bfloat16)
            grad_reset_state = contract_last(grad_cand_b, w_cand[...])
            grad_reset = grad_reset_state * state_f * reset_gate * (1.0 - reset_gate)
            gates_b = jnp.concatenate(
                [grad_reset.astype(jnp.bfloat16), grad_update.astype(jnp.bfloat16)], axis=1
            )
            state_grad[here, :] = (
                upstream * update_gate
                + grad_reset_state * reset_gate
                + contract_last(gates_b, w_state[...])
            ).astype(jnp.bfloat16)
            if with_grads:
                all_b = jnp.concatenate([gates_b, grad_cand_b], axis=1)
                grad_preact = contract_last(all_b, w_input[...]) * (1.0 - graph_out * graph_out)

                def add(at, value):
                    rows = pl.ds(at, value.shape[0])
                    grads[rows, :] += value

                add(0, contract_first(summed_b, grad_preact.astype(jnp.bfloat16)))
                to_input = contract_first(graph_b, all_b)
                for n in range(3):
                    add((1 + n) * width, to_input[:, n * width : (n + 1) * width])
                to_state = contract_first(state, gates_b)
                for n in range(2):
                    add((4 + n) * width, to_state[:, n * width : (n + 1) * width])
                add(6 * width, contract_first(reset_state, grad_cand_b))
                sums = [
                    jnp.sum(term, axis=0, keepdims=True)
                    for term in (grad_preact, grad_reset, grad_update, grad_cand_f)
                ]
                add(weight_rows, jnp.concatenate(sums + [jnp.zeros((4, width), jnp.float32)]))
            return carry

        lax.fori_loop(0, part_rows // ROW_BLOCK, step, 0)

    cell(own_base, True)

    to_mate = remote(
        grads_b.at[half(1 - core)], half_recv, pair_send.at[0], pair_recv.at[0], mate
    )
    across = [
        remote(
            half_b.at[quarter(rep_at(k))],
            rep_recv.at[k - 1],
            rep_send.at[k - 1],
            rep_got.at[k - 1],
            on_rep(k),
        )
        for k in range(1, reps)
    ]
    between = [
        remote(
            quarter_b.at[piece(chip_at(k))],
            chip_recv.at[k - 1],
            chip_send.at[k - 1],
            chip_got.at[k - 1],
            on_chip(k),
        )
        for k in range(1, chips)
    ]
    quarter_base = core * half_rows + rep * quarter_rows
    mine = pl.ds(pl.multiple_of(quarter_base + chip * piece_rows, piece_rows), piece_rows)
    my_quarter = pl.ds(pl.multiple_of(quarter_base, quarter_rows), quarter_rows)
    back_chip = [
        remote(
            final.at[mine], final.at[mine], chip_send2.at[k - 1], chip_got2.at[k - 1], on_chip(k)
        )
        for k in range(1, chips)
    ]
    back_rep = [
        remote(
            final.at[my_quarter],
            final.at[my_quarter],
            rep_send2.at[k - 1],
            rep_got2.at[k - 1],
            on_rep(k),
        )
        for k in range(1, reps)
    ]
    back_mate = remote(
        final.at[half(core)], final.at[half(core)], pair_send.at[1], pair_recv.at[1], mate
    )

    def stage_pair():
        to_mate.wait()
        half_b[...] = (grads[half(core), :] + half_recv[...].astype(jnp.float32)).astype(
            jnp.bfloat16
        )
        for copy in across:
            copy.start()

    def stage_rep():
        for copy in across:
            copy.wait()
        total = half_b[quarter(rep), :].astype(jnp.float32)
        for k in range(reps - 1):
            total = total + rep_recv[k].astype(jnp.float32)
        quarter_b[...] = total.astype(jnp.bfloat16)
        for copy in between:
            copy.start()

    def stage_chip():
        for copy in between:
            copy.wait()
        total = quarter_b[piece(chip), :].astype(jnp.float32)
        for k in range(chips - 1):
            total = total + chip_recv[k].astype(jnp.float32)
        final[mine, :] = (total * scale).astype(jnp.bfloat16)
        for copy in back_chip:
            copy.start()

    def stage_back_chip():
        for copy in back_chip:
            copy.wait()
        for copy in back_rep:
            copy.start()

    def stage_back_rep():
        for copy in back_rep:
            copy.wait()
        back_mate.start()

    grads_b[...] = grads[...].astype(jnp.bfloat16)
    to_mate.start()
    stage_pair()
    stages = [stage_rep, stage_chip, stage_back_chip, stage_back_rep]
    for k in range(1, reps):
        gather[k - 1].wait()
        cell(rep_origin(rep, reps, k) * part_rows, False)
        if stages:
            stages.pop(0)()
    for stage in stages:
        stage()
    back_mate.wait()
    grads_out[...] = final[...]


def unpack_kernel(
    state_in,
    back_in,
    final,
    new_state,
    state_grad,
    grad_graph,
    graph_bias,
    grad_input,
    grad_state,
    grad_cand,
    gate_sums,
):
    new_state[...] = state_in[...]
    state_grad[...] = back_in[...]

    @pl.when(pl.program_id(0) == 0)
    def _():
        width = grad_cand.shape[0]

        def take(at, count):
            return final[pl.ds(at, count), :].astype(jnp.float32)

        grad_graph[...] = take(0, width)
        for n in range(3):
            grad_input[:, n * width : (n + 1) * width] = take((1 + n) * width, width)
        for n in range(2):
            grad_state[:, n * width : (n + 1) * width] = take((4 + n) * width, width)
        grad_cand[...] = take(6 * width, width)
        bias = take(7 * width, 16)
        graph_bias[...] = bias[0]
        for n in range(3):
            gate_sums[n * width : (n + 1) * width] = bias[1 + n]


def unpack(new_state, state_grad, final, width):
    node_rows = new_state.shape[0]
    rows = node_rows // 4
    f32, b16 = jnp.float32, jnp.bfloat16
    shape = jax.ShapeDtypeStruct
    block = pl.BlockSpec((rows, width), lambda i: (i, 0))
    whole = pl.BlockSpec(memory_space=pltpu.VMEM)
    return pl.pallas_call(
        unpack_kernel,
        grid=(node_rows // rows,),
        out_shape=[
            shape((node_rows, width), b16),
            shape((node_rows, width), b16),
            shape((width, width), f32),
            shape((width,), f32),
            shape((width, 3 * width), f32),
            shape((width, 2 * width), f32),
            shape((width, width), f32),
            shape((3 * width,), f32),
        ],
        in_specs=[block, block, whole],
        out_specs=[block, block] + [whole] * 6,
        compiler_params=pltpu.CompilerParams(vmem_limit_bytes=VMEM_LIMIT),
    )(new_state, state_grad, final)


def cell_step(partial, first_half, state, cotangent, weights, chips, reps):
    node_rows, width = state.shape
    lanes = partial.shape[1]
    blks = chips * 2
    unit = 16 * blks * reps
    grad_rows = (7 * width + 16 + unit - 1) // unit * unit
    half_rows = grad_rows // 2
    quarter_rows = half_rows // reps
    piece_rows = quarter_rows // chips
    part_rows = node_rows // reps
    scale = float(node_rows * blks) ** (-0.5)
    f32, b16 = jnp.float32, jnp.bfloat16
    shape = jax.ShapeDtypeStruct
    whole = pl.BlockSpec(memory_space=pltpu.VMEM)
    anywhere = pl.BlockSpec(memory_space=pl.ANY)
    dma = pltpu.SemaphoreType.DMA
    return pl.pallas_call(
        functools.partial(cell_kernel, chips, reps, scale),
        out_shape=[
            shape((node_rows, width), b16),
            shape((node_rows, width), b16),
            shape((grad_rows, width), b16),
        ],
        in_specs=[anywhere, whole, anywhere, anywhere] + [whole] * 6,
        out_specs=[whole] * 3,
        scratch_shapes=[
            pltpu.VMEM((node_rows, width), b16),
            pltpu.VMEM((node_rows, width), b16),
            pltpu.VMEM((node_rows, lanes), b16),
            pltpu.VMEM((part_rows, lanes), b16),
            pltpu.VMEM((reps - 1, part_rows, lanes), b16),
            pltpu.VMEM((grad_rows, width), f32),
            pltpu.VMEM((grad_rows, width), b16),
            pltpu.VMEM((half_rows, width), b16),
            pltpu.VMEM((half_rows, width), b16),
            pltpu.VMEM((reps - 1, quarter_rows, width), b16),
            pltpu.VMEM((quarter_rows, width), b16),
            pltpu.VMEM((chips - 1, piece_rows, width), b16),
            pltpu.VMEM((grad_rows, width), b16),
            dma((3,)),
            dma((reps - 1,)),
            dma((reps - 1,)),
            dma((reps - 1,)),
            dma((reps - 1,)),
            dma((2,)),
            dma((2,)),
            dma((chips - 1,)),
            dma((chips - 1,)),
            dma((reps - 1,)),
            dma((reps - 1,)),
            dma((chips - 1,)),
            dma((chips - 1,)),
            dma((reps - 1,)),
            dma((reps - 1,)),
        ],
        compiler_params=pltpu.CompilerParams(
            collective_id=1, has_side_effects=True, vmem_limit_bytes=VMEM_LIMIT
        ),
    )(partial, first_half, state, cotangent, *weights)


def solution(mesh):
    chips = mesh.shape["blk"] // 2
    reps = mesh.shape["rep"]

    def local(
        features,
        state,
        tiles,
        tile_count,
        tile_rows,
        tile_cols,
        w_graph,
        b_graph,
        w_input,
        w_state,
        w_cand,
        b_gates,
        cotangent,
    ):
        per_rep = tiles.shape[1]
        lanes = features.shape[1] // 2
        lists = (tile_count, tile_rows, tile_cols, tiles[0])
        (sections,) = spread(features, None, 0, chips, reps, per_rep)
        partial = tile_products(*lists, sections)
        sections, first_half = spread(features, partial, lanes, chips, reps, per_rep)
        partial = tile_products(*lists, sections)
        weights = (w_graph, b_graph, w_input, w_state, w_cand, b_gates)
        outs = cell_step(partial, first_half, state, cotangent, weights, chips, reps)
        return tuple(unpack(*outs, w_cand.shape[0]))

    in_specs = (
        P("blk", None),
        P("blk", None),
        P("blk", "rep", None, None, None),
        P("blk", "rep"),
        P("blk", "rep", None),
        P("blk", "rep", None),
        P(),
        P(),
        P(),
        P(),
        P(),
        P(),
        P("blk", None),
    )
    out_specs = (P("blk", None), P("blk", None), P(), P(), P(), P(), P(), P())
    return jax.shard_map(local, mesh=mesh, in_specs=in_specs, out_specs=out_specs, check_vma=False)
```

```python
import functools

import jax
import jax.numpy as jnp
from jax import lax
from jax.experimental import pallas as pl
from jax.experimental.pallas import tpu as pltpu
from jax.sharding import PartitionSpec as P

MESH = pl.DeviceIdType.MESH
CHUNKS = 16
AHEAD = 3
GROUP = 8
ROW_BLOCK = 256
VMEM_LIMIT = 56 * 1024 * 1024


def contract_first(left, right):
    return lax.dot_general(
        left, right, (((0,), (0,)), ((), ())), preferred_element_type=jnp.float32
    )


def contract_last(left, right):
    return lax.dot_general(
        left, right, (((1,), (1,)), ((), ())), preferred_element_type=jnp.float32
    )


def product(left, right):
    return jnp.dot(left, right, preferred_element_type=jnp.float32)


def rep_shift(rep, reps, k):
    return ((rep // 2 + k // 2) % (reps // 2)) * 2 + (rep % 2 + k % 2) % 2


def rep_origin(rep, reps, k):
    return ((rep // 2 + reps // 2 - k // 2) % (reps // 2)) * 2 + (rep % 2 + k % 2) % 2


def spread_kernel(chips, reps, lane, reduces, *refs):
    if reduces:
        feat, partial, early, out, s_all = refs[:5]
        sems = refs[5:]
        part_own, part_recv, part_sem, rs_send, rs_recv, ag_send, ag_recv = sems[6:]
    else:
        feat, out, early = refs[:3]
        sems = refs[3:]
        early_up, early_down, early_recv, early_own = sems[6:]
    up_sem, down_sem, recv_sem, pair_sem, pair_recv, own_sem = sems[:6]
    blk = lax.axis_index("blk")
    rep = lax.axis_index("rep")
    core = blk % 2
    chip = blk // 2
    above = (chip + 1) % chips
    below = (chip + chips - 1) % chips
    chunk = feat.shape[0] // CHUNKS
    lanes = out.shape[2]
    is_owner = chip == rep
    not_owner = chip != rep
    has_up = jnp.logical_and(chip >= rep, chip < chips - 1)
    has_down = jnp.logical_and(chip <= rep, chip > 0)
    away = jnp.maximum(chip - rep, rep - chip)

    def ahead(hop):
        return jnp.minimum(jnp.maximum(AHEAD * (chips - 2 - hop), 0), CHUNKS)

    sent = ahead(away)
    held = ahead(away - 1)

    def rows_of(j):
        return pl.ds(pl.multiple_of(j * chunk, chunk), chunk)

    def own(j):
        return pltpu.make_async_copy(
            feat.at[rows_of(j), pl.ds(lane, lanes)], out.at[core, rows_of(j)], own_sem.at[j]
        )

    def load(j, carry):
        own(j).start()
        return carry

    @pl.when(is_owner)
    def _():
        lax.fori_loop(0, CHUNKS, load, 0)

    if reduces:
        def held_copy(j):
            return pltpu.make_async_copy(
                early.at[rows_of(j)], out.at[core, rows_of(j)], own_sem.at[j]
            )

        def load_held(j, carry):
            held_copy(j).start()
            return carry

        @pl.when(not_owner)
        def _():
            lax.fori_loop(0, held, load_held, 0)

    else:
        def early_load(j):
            return pltpu.make_async_copy(
                feat.at[rows_of(j), pl.ds(lane + lanes, lanes)],
                early.at[rows_of(j)],
                early_own.at[j],
            )

        def load_early(j, carry):
            early_load(j).start()
            return carry

        @pl.when(is_owner)
        def _():
            lax.fori_loop(0, sent, load_early, 0)

    def remote(src, dst, send_sem, recv_sem, target):
        return pltpu.make_async_remote_copy(
            src_ref=src,
            dst_ref=dst,
            send_sem=send_sem,
            recv_sem=recv_sem,
            device_id=target,
            device_id_type=MESH,
        )

    def send(j, target, send_sem, got):
        here = out.at[core, rows_of(j)]
        return remote(here, here, send_sem.at[j], got.at[j], {"blk": target, "rep": rep})

    def up(j):
        return send(j, above * 2 + core, up_sem, recv_sem)

    def down(j):
        return send(j, below * 2 + core, down_sem, recv_sem)

    def pair(j):
        return send(j, chip * 2 + 1 - core, pair_sem, pair_recv)

    others = range(1, reps)
    targets = [
        {"blk": other, "rep": rep}
        for other in (above * 2 + core, below * 2 + core, chip * 2 + 1 - core)
    ]
    if reduces:
        targets += [{"blk": blk, "rep": rep_shift(rep, reps, k)} for k in others]
    barrier = pltpu.get_barrier_semaphore()
    for target in targets:
        pl.semaphore_signal(barrier, inc=1, device_id=target, device_id_type=MESH)
    pl.semaphore_wait(barrier, len(targets))

    if reduces:
        part_rows = partial.shape[0] // reps

        def part(index):
            return pl.ds(pl.multiple_of(index * part_rows, part_rows), part_rows)

        load_own = pltpu.make_async_copy(partial.at[part(rep)], part_own, part_sem)
        load_own.start()
        scatter = [
            remote(
                partial.at[part(rep_shift(rep, reps, k))],
                part_recv.at[k - 1],
                rs_send.at[k - 1],
                rs_recv.at[k - 1],
                {"blk": blk, "rep": rep_shift(rep, reps, k)},
            )
            for k in others
        ]
        gather = [
            remote(
                s_all.at[part(rep)],
                s_all.at[part(rep)],
                ag_send.at[k - 1],
                ag_recv.at[k - 1],
                {"blk": blk, "rep": rep_shift(rep, reps, k)},
            )
            for k in others
        ]
        for copy in reversed(scatter):
            copy.start()

    first = sent if reduces else 0
    ready = held if reduces else 0

    def step(j, carry):
        @pl.when(is_owner)
        def _():
            own(j).wait()

        if reduces:
            @pl.when(jnp.logical_and(not_owner, j < ready))
            def _():
                held_copy(j).wait()

        @pl.when(jnp.logical_and(not_owner, j >= ready))
        def _():
            up(j).wait_recv()

        @pl.when(jnp.logical_and(has_up, j >= first))
        def _():
            up(j).start()

        @pl.when(jnp.logical_and(has_down, j >= first))
        def _():
            down(j).start()

        pair(j).start()
        return carry

    if reduces:
        middle = jnp.where(is_owner, CHUNKS, jnp.minimum(CHUNKS, held + CHUNKS // 2))
    else:
        middle = CHUNKS
    lax.fori_loop(0, middle, step, 0)
    if not reduces:

        def early_to(j, target, send_sem):
            here = early.at[rows_of(j)]
            return remote(
                here, here, send_sem.at[j], early_recv.at[j], {"blk": target, "rep": rep}
            )

        def early_up_copy(j):
            return early_to(j, above * 2 + core, early_up)

        def early_down_copy(j):
            return early_to(j, below * 2 + core, early_down)

        def early_step(j, carry):
            @pl.when(is_owner)
            def _():
                early_load(j).wait()

            @pl.when(not_owner)
            def _():
                early_up_copy(j).wait_recv()

            @pl.when(jnp.logical_and(has_up, j < sent))
            def _():
                early_up_copy(j).start()

            @pl.when(jnp.logical_and(has_down, j < sent))
            def _():
                early_down_copy(j).start()

            return carry

        lax.fori_loop(0, jnp.where(is_owner, sent, held), early_step, 0)

        def early_finish(j, carry):
            @pl.when(has_up)
            def _():
                early_up_copy(j).wait_send()

            @pl.when(has_down)
            def _():
                early_down_copy(j).wait_send()

            return carry

    if reduces:
        load_own.wait()
        for copy in scatter:
            copy.wait()
        add_parts(part_own, part_recv, s_all, rep * part_rows)
        for copy in gather:
            copy.start()
        lax.fori_loop(middle, CHUNKS, step, 0)

    def finish(j, carry):
        @pl.when(jnp.logical_and(has_up, j >= first))
        def _():
            up(j).wait_send()

        @pl.when(jnp.logical_and(has_down, j >= first))
        def _():
            down(j).wait_send()

        pair(j).wait()
        return carry

    lax.fori_loop(0, CHUNKS, finish, 0)
    if reduces:
        for copy in gather:
            copy.wait()
    else:
        lax.fori_loop(0, sent, early_finish, 0)


def add_parts(part_own, part_recv, s_all, base):
    others, rows = part_recv.shape[:2]

    def step(i, carry):
        here = pl.ds(pl.multiple_of(i * ROW_BLOCK, ROW_BLOCK), ROW_BLOCK)
        total = part_own[here, :].astype(jnp.float32)
        for k in range(others):
            total = total + part_recv[k, here, :].astype(jnp.float32)
        there = pl.ds(pl.multiple_of(base + i * ROW_BLOCK, ROW_BLOCK), ROW_BLOCK)
        s_all[there, :] = total.astype(jnp.bfloat16)
        return carry

    lax.fori_loop(0, rows // ROW_BLOCK, step, 0)


def spread(features, partial, early, lane, chips, reps, per_rep):
    reduces = partial is not None
    node_rows, width = features.shape
    lanes = width // 2
    part_rows = node_rows // reps
    chunk_sem = pltpu.SemaphoreType.DMA((CHUNKS,))
    rep_sem = pltpu.SemaphoreType.DMA((reps - 1,))
    shape = jax.ShapeDtypeStruct
    anywhere = pl.BlockSpec(memory_space=pl.ANY)
    vmem = pl.BlockSpec(memory_space=pltpu.VMEM)
    args = [features]
    out_shape = [shape((per_rep, node_rows, lanes), features.dtype)]
    scratch = [chunk_sem] * 6
    if reduces:
        args += [partial, early]
        out_shape.append(shape((node_rows, lanes), features.dtype))
        scratch += [
            pltpu.VMEM((part_rows, lanes), jnp.bfloat16),
            pltpu.VMEM((reps - 1, part_rows, lanes), jnp.bfloat16),
            pltpu.SemaphoreType.DMA(()),
            rep_sem,
            rep_sem,
            rep_sem,
            rep_sem,
        ]
    else:
        out_shape.append(shape((node_rows, lanes), features.dtype))
        scratch += [chunk_sem] * 4
    return pl.pallas_call(
        functools.partial(spread_kernel, chips, reps, lane, reduces),
        out_shape=out_shape,
        in_specs=[anywhere] * len(args),
        out_specs=[vmem] * len(out_shape),
        scratch_shapes=scratch,
        compiler_params=pltpu.CompilerParams(
            collective_id=2 if reduces else 0, has_side_effects=True, vmem_limit_bytes=VMEM_LIMIT
        ),
    )(*args)


def tiles_kernel(count, rows, cols, tiles, sections, out, acc):
    slot = pl.program_id(0)
    side = tiles.shape[2]

    @pl.when(slot == 0)
    def _():
        acc[...] = jnp.zeros_like(acc)

    used = count[0, slot]

    def step(g, carry):
        terms = []
        for i in range(GROUP):
            m = g * GROUP + i
            col = pl.multiple_of(cols[0, slot, m] * side, side)
            term = product(tiles[0, m], sections[0, pl.ds(col, side), :])
            terms.append(jnp.where(m < used, term, 0.0))
        for i in range(GROUP):
            row = pl.multiple_of(rows[0, slot, g * GROUP + i] * side, side)
            acc[pl.ds(row, side), :] += terms[i]
        return carry

    lax.fori_loop(0, (used + GROUP - 1) // GROUP, step, 0)

    @pl.when(slot == pl.num_programs(0) - 1)
    def _():
        out[...] = acc[...].astype(out.dtype)


def tile_products(count, rows, cols, tiles, sections):
    per_rep, cap, side = tiles.shape[:3]
    node_rows, width = sections.shape[1:]
    return pl.pallas_call(
        tiles_kernel,
        out_shape=jax.ShapeDtypeStruct((node_rows, width), jnp.bfloat16),
        grid_spec=pltpu.PrefetchScalarGridSpec(
            num_scalar_prefetch=3,
            grid=(per_rep,),
            in_specs=[
                pl.BlockSpec((1, cap, side, side), lambda s, *_: (s, 0, 0, 0)),
                pl.BlockSpec((1, node_rows, width), lambda s, *_: (s, 0, 0)),
            ],
            out_specs=pl.BlockSpec((node_rows, width), lambda s, *_: (0, 0)),
            scratch_shapes=[pltpu.VMEM((node_rows, width), jnp.float32)],
        ),
        compiler_params=pltpu.CompilerParams(vmem_limit_bytes=VMEM_LIMIT),
    )(count, rows, cols, tiles, sections)


def cell_kernel(
    chips,
    reps,
    scale,
    partial,
    first_half,
    state_hbm,
    cot_hbm,
    w_graph,
    b_graph,
    w_input,
    w_state,
    w_cand,
    b_gates,
    new_state,
    state_grad,
    grads_out,
    state_v,
    cot_v,
    s_all,
    part_own,
    part_recv,
    grads,
    grads_b,
    half_recv,
    half_b,
    rep_recv,
    quarter_b,
    chip_recv,
    final,
    local_sem,
    rs_send,
    rs_recv,
    ag_send,
    ag_recv,
    pair_send,
    pair_recv,
    chip_send,
    chip_got,
    rep_send,
    rep_got,
    chip_send2,
    chip_got2,
    rep_send2,
    rep_got2,
):
    blk = lax.axis_index("blk")
    rep = lax.axis_index("rep")
    core = blk % 2
    chip = blk // 2
    width = w_cand.shape[0]
    part_rows = partial.shape[0] // reps
    half_rows = half_b.shape[0]
    quarter_rows = quarter_b.shape[0]
    piece_rows = chip_recv.shape[1]
    weight_rows = 7 * width

    def rep_at(k):
        return rep_shift(rep, reps, k)

    def on_rep(k):
        return {"blk": blk, "rep": rep_at(k)}

    def chip_at(k):
        return (chip + k) % chips

    def on_chip(k):
        return {"blk": chip_at(k) * 2 + core, "rep": rep}

    mate = {"blk": chip * 2 + 1 - core, "rep": rep}

    def part(index):
        return pl.ds(pl.multiple_of(index * part_rows, part_rows), part_rows)

    def piece(index):
        return pl.ds(pl.multiple_of(index * piece_rows, piece_rows), piece_rows)

    def quarter(index):
        return pl.ds(pl.multiple_of(index * quarter_rows, quarter_rows), quarter_rows)

    def half(index):
        return pl.ds(pl.multiple_of(index * half_rows, half_rows), half_rows)

    def remote(src, dst, send_sem, recv_sem, target):
        return pltpu.make_async_remote_copy(
            src_ref=src,
            dst_ref=dst,
            send_sem=send_sem,
            recv_sem=recv_sem,
            device_id=target,
            device_id_type=MESH,
        )

    loads = [
        pltpu.make_async_copy(partial.at[part(rep)], part_own, local_sem.at[0]),
        pltpu.make_async_copy(state_hbm, state_v, local_sem.at[1]),
        pltpu.make_async_copy(cot_hbm, cot_v, local_sem.at[2]),
    ]
    for load in loads:
        load.start()

    barrier = pltpu.get_barrier_semaphore()
    targets = [on_rep(k) for k in range(1, reps)] + [on_chip(k) for k in range(1, chips)] + [mate]
    for target in targets:
        pl.semaphore_signal(barrier, inc=1, device_id=target, device_id_type=MESH)
    pl.semaphore_wait(barrier, len(targets))

    own_base = rep * part_rows
    blocks = part_rows // ROW_BLOCK

    def block(base, i):
        return pl.ds(pl.multiple_of(base + i * ROW_BLOCK, ROW_BLOCK), ROW_BLOCK)

    def scatter(k, i):
        return remote(
            partial.at[block(rep_at(k) * part_rows, i)],
            part_recv.at[k - 1, block(0, i)],
            rs_send.at[k - 1, i],
            rs_recv.at[k - 1, i],
            on_rep(k),
        )

    def gather(k, i):
        rows = block(own_base, i)
        return remote(
            s_all.at[rows], s_all.at[rows], ag_send.at[k - 1, i], ag_recv.at[k - 1, i], on_rep(k)
        )

    def send_parts(i, carry):
        for k in reversed(range(1, reps)):
            scatter(k, i).start()
        return carry

    lax.fori_loop(0, blocks, send_parts, 0)
    grads[...] = jnp.zeros_like(grads)
    for load in loads:
        load.wait()

    def add_block(i):
        for k in range(1, reps):
            scatter(k, i).wait()
        here = block(0, i)
        total = part_own[here, :].astype(jnp.float32)
        for k in range(reps - 1):
            total = total + part_recv[k, here, :].astype(jnp.float32)
        s_all[block(own_base, i), :] = total.astype(jnp.bfloat16)
        for k in range(1, reps):
            gather(k, i).start()

    def cell(base, before, with_grads):
        def step(i, carry):
            before(i)
            here = block(base, i)
            summed_b = jnp.concatenate([first_half[here, :], s_all[here, :]], axis=1)
            state = state_v[here, :]
            graph_out = jnp.tanh(product(summed_b, w_graph[...]) + b_graph[...].reshape(1, -1))
            graph_b = graph_out.astype(jnp.bfloat16)
            from_input = product(graph_b, w_input[...]) + b_gates[...].reshape(1, -1)
            from_state = product(state, w_state[...])
            reset_gate = jax.nn.sigmoid(from_input[:, :width] + from_state[:, :width])
            update_gate = jax.nn.sigmoid(from_input[:, width : 2 * width] + from_state[:, width:])
            state_f = state.astype(jnp.float32)
            reset_state = (reset_gate * state_f).astype(jnp.bfloat16)
            candidate = jnp.tanh(from_input[:, 2 * width :] + product(reset_state, w_cand[...]))
            keep = 1.0 - update_gate
            new_state[here, :] = (update_gate * state_f + keep * candidate).astype(jnp.bfloat16)
            upstream = cot_v[here, :].astype(jnp.float32)
            grad_update = upstream * (state_f - candidate) * update_gate * keep
            grad_cand_f = upstream * keep * (1.0 - candidate * candidate)
            grad_cand_b = grad_cand_f.astype(jnp.bfloat16)
            grad_reset_state = contract_last(grad_cand_b, w_cand[...])
            grad_reset = grad_reset_state * state_f * reset_gate * (1.0 - reset_gate)
            gates_b = jnp.concatenate(
                [grad_reset.astype(jnp.bfloat16), grad_update.astype(jnp.bfloat16)], axis=1
            )
            state_grad[here, :] = (
                upstream * update_gate
                + grad_reset_state * reset_gate
                + contract_last(gates_b, w_state[...])
            ).astype(jnp.bfloat16)
            if with_grads:
                all_b = jnp.concatenate([gates_b, grad_cand_b], axis=1)
                grad_preact = contract_last(all_b, w_input[...]) * (1.0 - graph_out * graph_out)

                def add(at, value):
                    rows = pl.ds(at, value.shape[0])
                    grads[rows, :] += value

                add(0, contract_first(summed_b, grad_preact.astype(jnp.bfloat16)))
                to_input = contract_first(graph_b, all_b)
                for n in range(3):
                    add((1 + n) * width, to_input[:, n * width : (n + 1) * width])
                to_state = contract_first(state, gates_b)
                for n in range(2):
                    add((4 + n) * width, to_state[:, n * width : (n + 1) * width])
                add(6 * width, contract_first(reset_state, grad_cand_b))
                sums = [
                    jnp.sum(term, axis=0, keepdims=True)
                    for term in (grad_preact, grad_reset, grad_update, grad_cand_f)
                ]
                add(weight_rows, jnp.concatenate(sums + [jnp.zeros((4, width), jnp.float32)]))
            return carry

        lax.fori_loop(0, blocks, step, 0)

    cell(own_base, add_block, True)

    to_mate = remote(
        grads_b.at[half(1 - core)], half_recv, pair_send.at[0], pair_recv.at[0], mate
    )
    across = [
        remote(
            half_b.at[quarter(rep_at(k))],
            rep_recv.at[k - 1],
            rep_send.at[k - 1],
            rep_got.at[k - 1],
            on_rep(k),
        )
        for k in range(1, reps)
    ]
    between = [
        remote(
            quarter_b.at[piece(chip_at(k))],
            chip_recv.at[k - 1],
            chip_send.at[k - 1],
            chip_got.at[k - 1],
            on_chip(k),
        )
        for k in range(1, chips)
    ]
    quarter_base = core * half_rows + rep * quarter_rows
    mine = pl.ds(pl.multiple_of(quarter_base + chip * piece_rows, piece_rows), piece_rows)
    my_quarter = pl.ds(pl.multiple_of(quarter_base, quarter_rows), quarter_rows)
    back_chip = [
        remote(
            final.at[mine], final.at[mine], chip_send2.at[k - 1], chip_got2.at[k - 1], on_chip(k)
        )
        for k in range(1, chips)
    ]
    back_rep = [
        remote(
            final.at[my_quarter],
            final.at[my_quarter],
            rep_send2.at[k - 1],
            rep_got2.at[k - 1],
            on_rep(k),
        )
        for k in range(1, reps)
    ]

    def back_mate(k):
        base = core * half_rows + rep_origin(rep, reps, k) * quarter_rows
        rows = pl.ds(pl.multiple_of(base, quarter_rows), quarter_rows)
        return remote(
            final.at[rows], final.at[rows], pair_send.at[1 + k], pair_recv.at[1 + k], mate
        )

    def stage_pair():
        to_mate.wait()
        half_b[...] = (grads[half(core), :] + half_recv[...].astype(jnp.float32)).astype(
            jnp.bfloat16
        )
        for copy in across:
            copy.start()

    def stage_rep():
        for copy in across:
            copy.wait()
        total = half_b[quarter(rep), :].astype(jnp.float32)
        for k in range(reps - 1):
            total = total + rep_recv[k].astype(jnp.float32)
        quarter_b[...] = total.astype(jnp.bfloat16)
        for copy in between:
            copy.start()

    def stage_chip():
        for copy in between:
            copy.wait()
        total = quarter_b[piece(chip), :].astype(jnp.float32)
        for k in range(chips - 1):
            total = total + chip_recv[k].astype(jnp.float32)
        final[mine, :] = (total * scale).astype(jnp.bfloat16)
        for copy in back_chip:
            copy.start()

    def stage_back_chip():
        for copy in back_chip:
            copy.wait()
        for copy in back_rep:
            copy.start()
        back_mate(0).start()

    def stage_back_rep():
        for k in range(1, reps):
            back_rep[k - 1].wait()
            back_mate(k).start()

    grads_b[...] = grads[...].astype(jnp.bfloat16)
    to_mate.start()
    stage_pair()
    stages = [stage_rep, stage_chip, stage_back_chip, stage_back_rep]
    for k in range(1, reps):
        cell(rep_origin(rep, reps, k) * part_rows, lambda i: gather(k, i).wait(), False)
        if stages:
            stages.pop(0)()
    for stage in stages:
        stage()
    for k in range(reps):
        back_mate(k).wait()
    grads_out[...] = final[...]


def unpack_kernel(
    state_in,
    back_in,
    final,
    new_state,
    state_grad,
    grad_graph,
    graph_bias,
    grad_input,
    grad_state,
    grad_cand,
    gate_sums,
):
    new_state[...] = state_in[...]
    state_grad[...] = back_in[...]

    @pl.when(pl.program_id(0) == 0)
    def _():
        width = grad_cand.shape[0]

        def take(at, count):
            return final[pl.ds(at, count), :].astype(jnp.float32)

        grad_graph[...] = take(0, width)
        for n in range(3):
            grad_input[:, n * width : (n + 1) * width] = take((1 + n) * width, width)
        for n in range(2):
            grad_state[:, n * width : (n + 1) * width] = take((4 + n) * width, width)
        grad_cand[...] = take(6 * width, width)
        bias = take(7 * width, 16)
        graph_bias[...] = bias[0]
        for n in range(3):
            gate_sums[n * width : (n + 1) * width] = bias[1 + n]


def unpack(new_state, state_grad, final, width):
    node_rows = new_state.shape[0]
    rows = node_rows // 2
    f32, b16 = jnp.float32, jnp.bfloat16
    shape = jax.ShapeDtypeStruct
    block = pl.BlockSpec((rows, width), lambda i: (i, 0))
    whole = pl.BlockSpec(memory_space=pltpu.VMEM)
    return pl.pallas_call(
        unpack_kernel,
        grid=(node_rows // rows,),
        out_shape=[
            shape((node_rows, width), b16),
            shape((node_rows, width), b16),
            shape((width, width), f32),
            shape((width,), f32),
            shape((width, 3 * width), f32),
            shape((width, 2 * width), f32),
            shape((width, width), f32),
            shape((3 * width,), f32),
        ],
        in_specs=[block, block, whole],
        out_specs=[block, block] + [whole] * 6,
        compiler_params=pltpu.CompilerParams(vmem_limit_bytes=VMEM_LIMIT),
    )(new_state, state_grad, final)


def cell_step(partial, first_half, state, cotangent, weights, chips, reps):
    node_rows, width = state.shape
    lanes = partial.shape[1]
    blks = chips * 2
    unit = 16 * blks * reps
    grad_rows = (7 * width + 16 + unit - 1) // unit * unit
    half_rows = grad_rows // 2
    quarter_rows = half_rows // reps
    piece_rows = quarter_rows // chips
    part_rows = node_rows // reps
    scale = float(node_rows * blks) ** (-0.5)
    f32, b16 = jnp.float32, jnp.bfloat16
    shape = jax.ShapeDtypeStruct
    whole = pl.BlockSpec(memory_space=pltpu.VMEM)
    anywhere = pl.BlockSpec(memory_space=pl.ANY)
    dma = pltpu.SemaphoreType.DMA
    return pl.pallas_call(
        functools.partial(cell_kernel, chips, reps, scale),
        out_shape=[
            shape((node_rows, width), b16),
            shape((node_rows, width), b16),
            shape((grad_rows, width), b16),
        ],
        in_specs=[anywhere, whole, anywhere, anywhere] + [whole] * 6,
        out_specs=[whole] * 3,
        scratch_shapes=[
            pltpu.VMEM((node_rows, width), b16),
            pltpu.VMEM((node_rows, width), b16),
            pltpu.VMEM((node_rows, lanes), b16),
            pltpu.VMEM((part_rows, lanes), b16),
            pltpu.VMEM((reps - 1, part_rows, lanes), b16),
            pltpu.VMEM((grad_rows, width), f32),
            pltpu.VMEM((grad_rows, width), b16),
            pltpu.VMEM((half_rows, width), b16),
            pltpu.VMEM((half_rows, width), b16),
            pltpu.VMEM((reps - 1, quarter_rows, width), b16),
            pltpu.VMEM((quarter_rows, width), b16),
            pltpu.VMEM((chips - 1, piece_rows, width), b16),
            pltpu.VMEM((grad_rows, width), b16),
            dma((3,)),
            dma((reps - 1, part_rows // ROW_BLOCK)),
            dma((reps - 1, part_rows // ROW_BLOCK)),
            dma((reps - 1, part_rows // ROW_BLOCK)),
            dma((reps - 1, part_rows // ROW_BLOCK)),
            dma((1 + reps,)),
            dma((1 + reps,)),
            dma((chips - 1,)),
            dma((chips - 1,)),
            dma((reps - 1,)),
            dma((reps - 1,)),
            dma((chips - 1,)),
            dma((chips - 1,)),
            dma((reps - 1,)),
            dma((reps - 1,)),
        ],
        compiler_params=pltpu.CompilerParams(
            collective_id=1, has_side_effects=True, vmem_limit_bytes=VMEM_LIMIT
        ),
    )(partial, first_half, state, cotangent, *weights)


def solution(mesh):
    chips = mesh.shape["blk"] // 2
    reps = mesh.shape["rep"]

    def local(
        features,
        state,
        tiles,
        tile_count,
        tile_rows,
        tile_cols,
        w_graph,
        b_graph,
        w_input,
        w_state,
        w_cand,
        b_gates,
        cotangent,
    ):
        per_rep = tiles.shape[1]
        lanes = features.shape[1] // 2
        lists = (tile_count, tile_rows, tile_cols, tiles[0])
        sections, early = spread(features, None, None, 0, chips, reps, per_rep)
        partial = tile_products(*lists, sections)
        sections, first_half = spread(
            features, partial, early, lanes, chips, reps, per_rep
        )
        partial = tile_products(*lists, sections)
        weights = (w_graph, b_graph, w_input, w_state, w_cand, b_gates)
        outs = cell_step(partial, first_half, state, cotangent, weights, chips, reps)
        return tuple(unpack(*outs, w_cand.shape[0]))

    in_specs = (
        P("blk", None),
        P("blk", None),
        P("blk", "rep", None, None, None),
        P("blk", "rep"),
        P("blk", "rep", None),
        P("blk", "rep", None),
        P(),
        P(),
        P(),
        P(),
        P(),
        P(),
        P("blk", None),
    )
    out_specs = (P("blk", None), P("blk", None), P(), P(), P(), P(), P(), P())
    return jax.shard_map(local, mesh=mesh, in_specs=in_specs, out_specs=out_specs, check_vma=False)
```

```python
import functools

import jax
import jax.numpy as jnp
from jax import lax
from jax.experimental import pallas as pl
from jax.experimental.pallas import tpu as pltpu
from jax.sharding import PartitionSpec as P

MESH = pl.DeviceIdType.MESH
CHUNKS = 16
AHEAD = 3
GROUP = 8
ROW_BLOCK = 256
VMEM_LIMIT = 56 * 1024 * 1024


def contract_first(left, right):
    return lax.dot_general(
        left, right, (((0,), (0,)), ((), ())), preferred_element_type=jnp.float32
    )


def contract_last(left, right):
    return lax.dot_general(
        left, right, (((1,), (1,)), ((), ())), preferred_element_type=jnp.float32
    )


def product(left, right):
    return jnp.dot(left, right, preferred_element_type=jnp.float32)


def rep_shift(rep, reps, k):
    return ((rep // 2 + k // 2) % (reps // 2)) * 2 + (rep % 2 + k % 2) % 2


def rep_origin(rep, reps, k):
    return ((rep // 2 + reps // 2 - k // 2) % (reps // 2)) * 2 + (rep % 2 + k % 2) % 2


def spread_kernel(chips, reps, lane, reduces, *refs):
    if reduces:
        feat, partial, early, out, s_all = refs[:5]
        sems = refs[5:]
        part_own, part_recv, part_sem, rs_send, rs_recv, ag_send, ag_recv = sems[6:]
    else:
        feat, out, early = refs[:3]
        sems = refs[3:]
        early_up, early_down, early_recv, early_own = sems[6:]
    up_sem, down_sem, recv_sem, pair_sem, pair_recv, own_sem = sems[:6]
    blk = lax.axis_index("blk")
    rep = lax.axis_index("rep")
    core = blk % 2
    chip = blk // 2
    above = (chip + 1) % chips
    below = (chip + chips - 1) % chips
    chunk = feat.shape[0] // CHUNKS
    lanes = out.shape[2]
    is_owner = chip == rep
    not_owner = chip != rep
    has_up = jnp.logical_and(chip >= rep, chip < chips - 1)
    has_down = jnp.logical_and(chip <= rep, chip > 0)
    away = jnp.maximum(chip - rep, rep - chip)

    def ahead(hop):
        return jnp.minimum(jnp.maximum(AHEAD * (chips - 2 - hop), 0), CHUNKS)

    sent = ahead(away)
    held = ahead(away - 1)

    def rows_of(j):
        return pl.ds(pl.multiple_of(j * chunk, chunk), chunk)

    def own(j):
        return pltpu.make_async_copy(
            feat.at[rows_of(j), pl.ds(lane, lanes)], out.at[core, rows_of(j)], own_sem.at[j]
        )

    def load(j, carry):
        own(j).start()
        return carry

    @pl.when(is_owner)
    def _():
        lax.fori_loop(0, CHUNKS, load, 0)

    if reduces:
        def held_copy(j):
            return pltpu.make_async_copy(
                early.at[rows_of(j)], out.at[core, rows_of(j)], own_sem.at[j]
            )

        def load_held(j, carry):
            held_copy(j).start()
            return carry

        @pl.when(not_owner)
        def _():
            lax.fori_loop(0, held, load_held, 0)

    else:
        def early_load(j):
            return pltpu.make_async_copy(
                feat.at[rows_of(j), pl.ds(lane + lanes, lanes)],
                early.at[rows_of(j)],
                early_own.at[j],
            )

        def load_early(j, carry):
            early_load(j).start()
            return carry

        @pl.when(is_owner)
        def _():
            lax.fori_loop(0, sent, load_early, 0)

    def remote(src, dst, send_sem, recv_sem, target):
        return pltpu.make_async_remote_copy(
            src_ref=src,
            dst_ref=dst,
            send_sem=send_sem,
            recv_sem=recv_sem,
            device_id=target,
            device_id_type=MESH,
        )

    def send(j, target, send_sem, got):
        here = out.at[core, rows_of(j)]
        return remote(here, here, send_sem.at[j], got.at[j], {"blk": target, "rep": rep})

    def up(j):
        return send(j, above * 2 + core, up_sem, recv_sem)

    def down(j):
        return send(j, below * 2 + core, down_sem, recv_sem)

    def pair(j):
        return send(j, chip * 2 + 1 - core, pair_sem, pair_recv)

    others = range(1, reps)
    targets = [
        {"blk": other, "rep": rep}
        for other in (above * 2 + core, below * 2 + core, chip * 2 + 1 - core)
    ]
    if reduces:
        targets += [{"blk": blk, "rep": rep_shift(rep, reps, k)} for k in others]
    barrier = pltpu.get_barrier_semaphore()
    for target in targets:
        pl.semaphore_signal(barrier, inc=1, device_id=target, device_id_type=MESH)
    pl.semaphore_wait(barrier, len(targets))

    if reduces:
        part_rows = partial.shape[0] // reps

        def part(index):
            return pl.ds(pl.multiple_of(index * part_rows, part_rows), part_rows)

        load_own = pltpu.make_async_copy(partial.at[part(rep)], part_own, part_sem)
        load_own.start()
        scatter = [
            remote(
                partial.at[part(rep_shift(rep, reps, k))],
                part_recv.at[k - 1],
                rs_send.at[k - 1],
                rs_recv.at[k - 1],
                {"blk": blk, "rep": rep_shift(rep, reps, k)},
            )
            for k in others
        ]
        gather = [
            remote(
                s_all.at[part(rep)],
                s_all.at[part(rep)],
                ag_send.at[k - 1],
                ag_recv.at[k - 1],
                {"blk": blk, "rep": rep_shift(rep, reps, k)},
            )
            for k in others
        ]
        for copy in reversed(scatter):
            copy.start()

    first = sent if reduces else 0
    ready = held if reduces else 0

    def step(j, carry):
        @pl.when(is_owner)
        def _():
            own(j).wait()

        if reduces:
            @pl.when(jnp.logical_and(not_owner, j < ready))
            def _():
                held_copy(j).wait()

        @pl.when(jnp.logical_and(not_owner, j >= ready))
        def _():
            up(j).wait_recv()

        @pl.when(jnp.logical_and(has_up, j >= first))
        def _():
            up(j).start()

        @pl.when(jnp.logical_and(has_down, j >= first))
        def _():
            down(j).start()

        pair(j).start()
        return carry

    if reduces:
        middle = jnp.where(is_owner, CHUNKS, jnp.minimum(CHUNKS, held + CHUNKS // 2))
    else:
        middle = CHUNKS
    lax.fori_loop(0, middle, step, 0)
    if not reduces:

        def early_to(j, target, send_sem):
            here = early.at[rows_of(j)]
            return remote(
                here, here, send_sem.at[j], early_recv.at[j], {"blk": target, "rep": rep}
            )

        def early_up_copy(j):
            return early_to(j, above * 2 + core, early_up)

        def early_down_copy(j):
            return early_to(j, below * 2 + core, early_down)

        def early_step(j, carry):
            @pl.when(is_owner)
            def _():
                early_load(j).wait()

            @pl.when(not_owner)
            def _():
                early_up_copy(j).wait_recv()

            @pl.when(jnp.logical_and(has_up, j < sent))
            def _():
                early_up_copy(j).start()

            @pl.when(jnp.logical_and(has_down, j < sent))
            def _():
                early_down_copy(j).start()

            return carry

        lax.fori_loop(0, jnp.where(is_owner, sent, held), early_step, 0)

        def early_finish(j, carry):
            @pl.when(has_up)
            def _():
                early_up_copy(j).wait_send()

            @pl.when(has_down)
            def _():
                early_down_copy(j).wait_send()

            return carry

    if reduces:
        load_own.wait()
        for copy in scatter:
            copy.wait()
        add_parts(part_own, part_recv, s_all, rep * part_rows)
        for copy in gather:
            copy.start()
        lax.fori_loop(middle, CHUNKS, step, 0)

    def finish(j, carry):
        @pl.when(jnp.logical_and(has_up, j >= first))
        def _():
            up(j).wait_send()

        @pl.when(jnp.logical_and(has_down, j >= first))
        def _():
            down(j).wait_send()

        pair(j).wait()
        return carry

    lax.fori_loop(0, CHUNKS, finish, 0)
    if reduces:
        for copy in gather:
            copy.wait()
    else:
        lax.fori_loop(0, sent, early_finish, 0)


def add_parts(part_own, part_recv, s_all, base):
    others, rows = part_recv.shape[:2]

    def step(i, carry):
        here = pl.ds(pl.multiple_of(i * ROW_BLOCK, ROW_BLOCK), ROW_BLOCK)
        total = part_own[here, :].astype(jnp.float32)
        for k in range(others):
            total = total + part_recv[k, here, :].astype(jnp.float32)
        there = pl.ds(pl.multiple_of(base + i * ROW_BLOCK, ROW_BLOCK), ROW_BLOCK)
        s_all[there, :] = total.astype(jnp.bfloat16)
        return carry

    lax.fori_loop(0, rows // ROW_BLOCK, step, 0)


def spread(features, partial, early, lane, chips, reps, per_rep):
    reduces = partial is not None
    node_rows, width = features.shape
    lanes = width // 2
    part_rows = node_rows // reps
    chunk_sem = pltpu.SemaphoreType.DMA((CHUNKS,))
    rep_sem = pltpu.SemaphoreType.DMA((reps - 1,))
    shape = jax.ShapeDtypeStruct
    anywhere = pl.BlockSpec(memory_space=pl.ANY)
    vmem = pl.BlockSpec(memory_space=pltpu.VMEM)
    args = [features]
    out_shape = [shape((per_rep, node_rows, lanes), features.dtype)]
    scratch = [chunk_sem] * 6
    if reduces:
        args += [partial, early]
        out_shape.append(shape((node_rows, lanes), features.dtype))
        scratch += [
            pltpu.VMEM((part_rows, lanes), jnp.bfloat16),
            pltpu.VMEM((reps - 1, part_rows, lanes), jnp.bfloat16),
            pltpu.SemaphoreType.DMA(()),
            rep_sem,
            rep_sem,
            rep_sem,
            rep_sem,
        ]
    else:
        out_shape.append(shape((node_rows, lanes), features.dtype))
        scratch += [chunk_sem] * 4
    return pl.pallas_call(
        functools.partial(spread_kernel, chips, reps, lane, reduces),
        out_shape=out_shape,
        in_specs=[anywhere] * len(args),
        out_specs=[vmem] * len(out_shape),
        scratch_shapes=scratch,
        compiler_params=pltpu.CompilerParams(
            collective_id=2 if reduces else 0, has_side_effects=True, vmem_limit_bytes=VMEM_LIMIT
        ),
    )(*args)


def tiles_kernel(count, rows, cols, tiles, sections, out, acc):
    slot = pl.program_id(0)
    span = pl.program_id(1)
    held, side = tiles.shape[1:3]
    base = span * held

    @pl.when(jnp.logical_and(slot == 0, span == 0))
    def _():
        acc[...] = jnp.zeros_like(acc)

    used = jnp.clip(count[0, slot] - base, 0, held)

    def step(g, carry):
        terms = []
        for i in range(GROUP):
            m = g * GROUP + i
            col = pl.multiple_of(cols[0, slot, base + m] * side, side)
            term = product(tiles[0, m], sections[0, pl.ds(col, side), :])
            terms.append(jnp.where(m < used, term, 0.0))
        for i in range(GROUP):
            row = pl.multiple_of(rows[0, slot, base + g * GROUP + i] * side, side)
            acc[pl.ds(row, side), :] += terms[i]
        return carry

    lax.fori_loop(0, (used + GROUP - 1) // GROUP, step, 0)

    @pl.when(jnp.logical_and(slot == pl.num_programs(0) - 1, span == pl.num_programs(1) - 1))
    def _():
        out[...] = acc[...].astype(out.dtype)


def tile_products(count, rows, cols, tiles, sections):
    per_rep, cap, side = tiles.shape[:3]
    node_rows, width = sections.shape[1:]
    return pl.pallas_call(
        tiles_kernel,
        out_shape=jax.ShapeDtypeStruct((node_rows, width), jnp.bfloat16),
        grid_spec=pltpu.PrefetchScalarGridSpec(
            num_scalar_prefetch=3,
            grid=(per_rep, 2),
            in_specs=[
                pl.BlockSpec((1, cap // 2, side, side), lambda s, h, *_: (s, h, 0, 0)),
                pl.BlockSpec((1, node_rows, width), lambda s, h, *_: (s, 0, 0)),
            ],
            out_specs=pl.BlockSpec((node_rows, width), lambda s, h, *_: (0, 0)),
            scratch_shapes=[pltpu.VMEM((node_rows, width), jnp.float32)],
        ),
        compiler_params=pltpu.CompilerParams(vmem_limit_bytes=VMEM_LIMIT),
    )(count, rows, cols, tiles, sections)


def cell_kernel(
    chips,
    reps,
    scale,
    partial,
    first_half,
    state_hbm,
    cot_hbm,
    w_graph,
    b_graph,
    w_input,
    w_state,
    w_cand,
    b_gates,
    new_state,
    state_grad,
    grads_out,
    state_v,
    cot_v,
    s_all,
    part_own,
    part_recv,
    grads,
    grads_b,
    half_recv,
    half_b,
    rep_recv,
    quarter_b,
    chip_recv,
    final,
    local_sem,
    rs_send,
    rs_recv,
    ag_send,
    ag_recv,
    pair_send,
    pair_recv,
    chip_send,
    chip_got,
    rep_send,
    rep_got,
    chip_send2,
    chip_got2,
    rep_send2,
    rep_got2,
):
    blk = lax.axis_index("blk")
    rep = lax.axis_index("rep")
    core = blk % 2
    chip = blk // 2
    width = w_cand.shape[0]
    part_rows = partial.shape[0] // reps
    half_rows = half_b.shape[0]
    quarter_rows = quarter_b.shape[0]
    piece_rows = chip_recv.shape[1]
    weight_rows = 7 * width

    def rep_at(k):
        return rep_shift(rep, reps, k)

    def on_rep(k):
        return {"blk": blk, "rep": rep_at(k)}

    def chip_at(k):
        return (chip + k) % chips

    def on_chip(k):
        return {"blk": chip_at(k) * 2 + core, "rep": rep}

    mate = {"blk": chip * 2 + 1 - core, "rep": rep}

    def part(index):
        return pl.ds(pl.multiple_of(index * part_rows, part_rows), part_rows)

    def piece(index):
        return pl.ds(pl.multiple_of(index * piece_rows, piece_rows), piece_rows)

    def quarter(index):
        return pl.ds(pl.multiple_of(index * quarter_rows, quarter_rows), quarter_rows)

    def half(index):
        return pl.ds(pl.multiple_of(index * half_rows, half_rows), half_rows)

    def remote(src, dst, send_sem, recv_sem, target):
        return pltpu.make_async_remote_copy(
            src_ref=src,
            dst_ref=dst,
            send_sem=send_sem,
            recv_sem=recv_sem,
            device_id=target,
            device_id_type=MESH,
        )

    loads = [
        pltpu.make_async_copy(partial.at[part(rep)], part_own, local_sem.at[0]),
        pltpu.make_async_copy(state_hbm, state_v, local_sem.at[1]),
        pltpu.make_async_copy(cot_hbm, cot_v, local_sem.at[2]),
    ]
    for load in loads:
        load.start()

    barrier = pltpu.get_barrier_semaphore()
    targets = [on_rep(k) for k in range(1, reps)] + [on_chip(k) for k in range(1, chips)] + [mate]
    for target in targets:
        pl.semaphore_signal(barrier, inc=1, device_id=target, device_id_type=MESH)
    pl.semaphore_wait(barrier, len(targets))

    own_base = rep * part_rows
    blocks = part_rows // ROW_BLOCK

    def block(base, i):
        return pl.ds(pl.multiple_of(base + i * ROW_BLOCK, ROW_BLOCK), ROW_BLOCK)

    def scatter(k, i):
        return remote(
            partial.at[block(rep_at(k) * part_rows, i)],
            part_recv.at[k - 1, block(0, i)],
            rs_send.at[k - 1, i],
            rs_recv.at[k - 1, i],
            on_rep(k),
        )

    def gather(k, i):
        rows = block(own_base, i)
        return remote(
            s_all.at[rows], s_all.at[rows], ag_send.at[k - 1, i], ag_recv.at[k - 1, i], on_rep(k)
        )

    def send_parts(i, carry):
        for k in reversed(range(1, reps)):
            scatter(k, i).start()
        return carry

    lax.fori_loop(0, blocks, send_parts, 0)
    grads[...] = jnp.zeros_like(grads)
    for load in loads:
        load.wait()

    def add_block(i):
        for k in range(1, reps):
            scatter(k, i).wait()
        here = block(0, i)
        total = part_own[here, :].astype(jnp.float32)
        for k in range(reps - 1):
            total = total + part_recv[k, here, :].astype(jnp.float32)
        s_all[block(own_base, i), :] = total.astype(jnp.bfloat16)
        for k in range(1, reps):
            gather(k, i).start()

    def cell(base, before, with_grads):
        def step(i, carry):
            before(i)
            here = block(base, i)
            summed_b = jnp.concatenate([first_half[here, :], s_all[here, :]], axis=1)
            state = state_v[here, :]
            graph_out = jnp.tanh(product(summed_b, w_graph[...]) + b_graph[...].reshape(1, -1))
            graph_b = graph_out.astype(jnp.bfloat16)
            from_input = product(graph_b, w_input[...]) + b_gates[...].reshape(1, -1)
            from_state = product(state, w_state[...])
            reset_gate = jax.nn.sigmoid(from_input[:, :width] + from_state[:, :width])
            update_gate = jax.nn.sigmoid(from_input[:, width : 2 * width] + from_state[:, width:])
            state_f = state.astype(jnp.float32)
            reset_state = (reset_gate * state_f).astype(jnp.bfloat16)
            candidate = jnp.tanh(from_input[:, 2 * width :] + product(reset_state, w_cand[...]))
            keep = 1.0 - update_gate
            new_state[here, :] = (update_gate * state_f + keep * candidate).astype(jnp.bfloat16)
            upstream = cot_v[here, :].astype(jnp.float32)
            grad_update = upstream * (state_f - candidate) * update_gate * keep
            grad_cand_f = upstream * keep * (1.0 - candidate * candidate)
            grad_cand_b = grad_cand_f.astype(jnp.bfloat16)
            grad_reset_state = contract_last(grad_cand_b, w_cand[...])
            grad_reset = grad_reset_state * state_f * reset_gate * (1.0 - reset_gate)
            gates_b = jnp.concatenate(
                [grad_reset.astype(jnp.bfloat16), grad_update.astype(jnp.bfloat16)], axis=1
            )
            state_grad[here, :] = (
                upstream * update_gate
                + grad_reset_state * reset_gate
                + contract_last(gates_b, w_state[...])
            ).astype(jnp.bfloat16)
            if with_grads:
                all_b = jnp.concatenate([gates_b, grad_cand_b], axis=1)
                grad_preact = contract_last(all_b, w_input[...]) * (1.0 - graph_out * graph_out)

                def add(at, value):
                    rows = pl.ds(at, value.shape[0])
                    grads[rows, :] += value

                add(0, contract_first(summed_b, grad_preact.astype(jnp.bfloat16)))
                to_input = contract_first(graph_b, all_b)
                for n in range(3):
                    add((1 + n) * width, to_input[:, n * width : (n + 1) * width])
                to_state = contract_first(state, gates_b)
                for n in range(2):
                    add((4 + n) * width, to_state[:, n * width : (n + 1) * width])
                add(6 * width, contract_first(reset_state, grad_cand_b))
                sums = [
                    jnp.sum(term, axis=0, keepdims=True)
                    for term in (grad_preact, grad_reset, grad_update, grad_cand_f)
                ]
                add(weight_rows, jnp.concatenate(sums + [jnp.zeros((4, width), jnp.float32)]))
            return carry

        lax.fori_loop(0, blocks, step, 0)

    cell(own_base, add_block, True)

    to_mate = remote(
        grads_b.at[half(1 - core)], half_recv, pair_send.at[0], pair_recv.at[0], mate
    )
    across = [
        remote(
            half_b.at[quarter(rep_at(k))],
            rep_recv.at[k - 1],
            rep_send.at[k - 1],
            rep_got.at[k - 1],
            on_rep(k),
        )
        for k in range(1, reps)
    ]
    between = [
        remote(
            quarter_b.at[piece(chip_at(k))],
            chip_recv.at[k - 1],
            chip_send.at[k - 1],
            chip_got.at[k - 1],
            on_chip(k),
        )
        for k in range(1, chips)
    ]
    quarter_base = core * half_rows + rep * quarter_rows
    mine = pl.ds(pl.multiple_of(quarter_base + chip * piece_rows, piece_rows), piece_rows)
    my_quarter = pl.ds(pl.multiple_of(quarter_base, quarter_rows), quarter_rows)
    back_chip = [
        remote(
            final.at[mine], final.at[mine], chip_send2.at[k - 1], chip_got2.at[k - 1], on_chip(k)
        )
        for k in range(1, chips)
    ]
    back_rep = [
        remote(
            final.at[my_quarter],
            final.at[my_quarter],
            rep_send2.at[k - 1],
            rep_got2.at[k - 1],
            on_rep(k),
        )
        for k in range(1, reps)
    ]

    def back_mate(k):
        base = core * half_rows + rep_origin(rep, reps, k) * quarter_rows
        rows = pl.ds(pl.multiple_of(base, quarter_rows), quarter_rows)
        return remote(
            final.at[rows], final.at[rows], pair_send.at[1 + k], pair_recv.at[1 + k], mate
        )

    def stage_pair():
        to_mate.wait()
        half_b[...] = (grads[half(core), :] + half_recv[...].astype(jnp.float32)).astype(
            jnp.bfloat16
        )
        for copy in across:
            copy.start()

    def stage_rep():
        for copy in across:
            copy.wait()
        total = half_b[quarter(rep), :].astype(jnp.float32)
        for k in range(reps - 1):
            total = total + rep_recv[k].astype(jnp.float32)
        quarter_b[...] = total.astype(jnp.bfloat16)
        for copy in between:
            copy.start()

    def stage_chip():
        for copy in between:
            copy.wait()
        total = quarter_b[piece(chip), :].astype(jnp.float32)
        for k in range(chips - 1):
            total = total + chip_recv[k].astype(jnp.float32)
        final[mine, :] = (total * scale).astype(jnp.bfloat16)
        for copy in back_chip:
            copy.start()

    def stage_back_chip():
        for copy in back_chip:
            copy.wait()
        for copy in back_rep:
            copy.start()
        back_mate(0).start()

    def stage_back_rep():
        for k in range(1, reps):
            back_rep[k - 1].wait()
            back_mate(k).start()

    grads_b[...] = grads[...].astype(jnp.bfloat16)
    to_mate.start()
    stage_pair()
    stages = [stage_rep, stage_chip, stage_back_chip, stage_back_rep]
    for k in range(1, reps):
        cell(rep_origin(rep, reps, k) * part_rows, lambda i: gather(k, i).wait(), False)
        if stages:
            stages.pop(0)()
    for stage in stages:
        stage()
    for k in range(reps):
        back_mate(k).wait()
    grads_out[...] = final[...]


def unpack_kernel(
    state_in,
    back_in,
    final,
    new_state,
    state_grad,
    grad_graph,
    graph_bias,
    grad_input,
    grad_state,
    grad_cand,
    gate_sums,
):
    new_state[...] = state_in[...]
    state_grad[...] = back_in[...]

    @pl.when(pl.program_id(0) == 0)
    def _():
        width = grad_cand.shape[0]

        def take(at, count):
            return final[pl.ds(at, count), :].astype(jnp.float32)

        grad_graph[...] = take(0, width)
        for n in range(3):
            grad_input[:, n * width : (n + 1) * width] = take((1 + n) * width, width)
        for n in range(2):
            grad_state[:, n * width : (n + 1) * width] = take((4 + n) * width, width)
        grad_cand[...] = take(6 * width, width)
        bias = take(7 * width, 16)
        graph_bias[...] = bias[0]
        for n in range(3):
            gate_sums[n * width : (n + 1) * width] = bias[1 + n]


def unpack(new_state, state_grad, final, width):
    node_rows = new_state.shape[0]
    rows = node_rows // 2
    f32, b16 = jnp.float32, jnp.bfloat16
    shape = jax.ShapeDtypeStruct
    block = pl.BlockSpec((rows, width), lambda i: (i, 0))
    whole = pl.BlockSpec(memory_space=pltpu.VMEM)
    return pl.pallas_call(
        unpack_kernel,
        grid=(node_rows // rows,),
        out_shape=[
            shape((node_rows, width), b16),
            shape((node_rows, width), b16),
            shape((width, width), f32),
            shape((width,), f32),
            shape((width, 3 * width), f32),
            shape((width, 2 * width), f32),
            shape((width, width), f32),
            shape((3 * width,), f32),
        ],
        in_specs=[block, block, whole],
        out_specs=[block, block] + [whole] * 6,
        compiler_params=pltpu.CompilerParams(vmem_limit_bytes=VMEM_LIMIT),
    )(new_state, state_grad, final)


def cell_step(partial, first_half, state, cotangent, weights, chips, reps):
    node_rows, width = state.shape
    lanes = partial.shape[1]
    blks = chips * 2
    unit = 16 * blks * reps
    grad_rows = (7 * width + 16 + unit - 1) // unit * unit
    half_rows = grad_rows // 2
    quarter_rows = half_rows // reps
    piece_rows = quarter_rows // chips
    part_rows = node_rows // reps
    scale = float(node_rows * blks) ** (-0.5)
    f32, b16 = jnp.float32, jnp.bfloat16
    shape = jax.ShapeDtypeStruct
    whole = pl.BlockSpec(memory_space=pltpu.VMEM)
    anywhere = pl.BlockSpec(memory_space=pl.ANY)
    dma = pltpu.SemaphoreType.DMA
    return pl.pallas_call(
        functools.partial(cell_kernel, chips, reps, scale),
        out_shape=[
            shape((node_rows, width), b16),
            shape((node_rows, width), b16),
            shape((grad_rows, width), b16),
        ],
        in_specs=[anywhere, whole, anywhere, anywhere] + [whole] * 6,
        out_specs=[whole] * 3,
        scratch_shapes=[
            pltpu.VMEM((node_rows, width), b16),
            pltpu.VMEM((node_rows, width), b16),
            pltpu.VMEM((node_rows, lanes), b16),
            pltpu.VMEM((part_rows, lanes), b16),
            pltpu.VMEM((reps - 1, part_rows, lanes), b16),
            pltpu.VMEM((grad_rows, width), f32),
            pltpu.VMEM((grad_rows, width), b16),
            pltpu.VMEM((half_rows, width), b16),
            pltpu.VMEM((half_rows, width), b16),
            pltpu.VMEM((reps - 1, quarter_rows, width), b16),
            pltpu.VMEM((quarter_rows, width), b16),
            pltpu.VMEM((chips - 1, piece_rows, width), b16),
            pltpu.VMEM((grad_rows, width), b16),
            dma((3,)),
            dma((reps - 1, part_rows // ROW_BLOCK)),
            dma((reps - 1, part_rows // ROW_BLOCK)),
            dma((reps - 1, part_rows // ROW_BLOCK)),
            dma((reps - 1, part_rows // ROW_BLOCK)),
            dma((1 + reps,)),
            dma((1 + reps,)),
            dma((chips - 1,)),
            dma((chips - 1,)),
            dma((reps - 1,)),
            dma((reps - 1,)),
            dma((chips - 1,)),
            dma((chips - 1,)),
            dma((reps - 1,)),
            dma((reps - 1,)),
        ],
        compiler_params=pltpu.CompilerParams(
            collective_id=1, has_side_effects=True, vmem_limit_bytes=VMEM_LIMIT
        ),
    )(partial, first_half, state, cotangent, *weights)


def solution(mesh):
    chips = mesh.shape["blk"] // 2
    reps = mesh.shape["rep"]

    def local(
        features,
        state,
        tiles,
        tile_count,
        tile_rows,
        tile_cols,
        w_graph,
        b_graph,
        w_input,
        w_state,
        w_cand,
        b_gates,
        cotangent,
    ):
        per_rep = tiles.shape[1]
        lanes = features.shape[1] // 2
        lists = (tile_count, tile_rows, tile_cols, tiles[0])
        sections, early = spread(features, None, None, 0, chips, reps, per_rep)
        partial = tile_products(*lists, sections)
        sections, first_half = spread(
            features, partial, early, lanes, chips, reps, per_rep
        )
        partial = tile_products(*lists, sections)
        weights = (w_graph, b_graph, w_input, w_state, w_cand, b_gates)
        outs = cell_step(partial, first_half, state, cotangent, weights, chips, reps)
        return tuple(unpack(*outs, w_cand.shape[0]))

    in_specs = (
        P("blk", None),
        P("blk", None),
        P("blk", "rep", None, None, None),
        P("blk", "rep"),
        P("blk", "rep", None),
        P("blk", "rep", None),
        P(),
        P(),
        P(),
        P(),
        P(),
        P(),
        P("blk", None),
    )
    out_specs = (P("blk", None), P("blk", None), P(), P(), P(), P(), P(), P())
    return jax.shard_map(local, mesh=mesh, in_specs=in_specs, out_specs=out_specs, check_vma=False)
```
